512 devices in a mesh: dp: 128 (over z, x, core), mp: 4 (over y).
Axes of the slice: x: 4, y: 4, z: 16, core: 2. Of those that a mesh axis runs over, the one named last changes fastest.
Arguments:
- old_factors: float32 [128, 1, 1024, 1024], P('dp', None, 'mp'), as said below
- gradients: bfloat16 [128, 56, 32, 1024], P('dp', None, 'mp'), may hold values from -2.5 to 2.5
- old_slots: int32 [128, 1], replicated, may hold values from -1 to 71, as said below
- new_slots: int32 [128, 1], replicated, may hold values from -1 to 71, as said below
Outputs:
- inverses: bfloat16 [128, 1, 1024, 1024], P('dp', None, 'mp')
- preconditioned: bfloat16 [56, 32, 1024], P(None, 'mp')
The draws below stay inside these ranges and needn't reach their ends.
Inputs may be any that keep to these rules, and one draw needn't show every extreme that they name: `old_slots`: every block number 0 to 71 stands in exactly one slot and all other slots hold -1; some owner has all 1 slots filled. `new_slots`: every block number 0 to 71 stands in exactly one slot and all other slots hold -1; some owner has all 1 slots filled. `old_factors`: every slot holds a symmetric positive definite matrix.
All inputs are finite; a program needn't handle non-finite values.
Results may differ from the reference program's by a relative error of at most 0.0057.
Values may be sent and summed in bfloat16 or wider, within the bound.
No kernel may reach another device: no remote copies, remote signals or barrier semaphores. Data moves between devices by JAX's collectives and lax.ppermute only.
A program may use at most 64 MiB of HBM per device.

```python
import math
import jax
import jax.numpy as jnp
from jax import lax

D = 8192
FF = 28672
BLK = 1024
LAYERS = 2
A_SPAN = 28
LAYER_BLOCKS = 36
BLOCKS = 72
TILES = 56
SLOTS = 1
ROWS_ALL = 32
N_DP = 128


def owner_plan(key):
    capacity = N_DP * SLOTS
    score_key, owner_key, block_key = jax.random.split(key, 3)
    scores = jax.random.permutation(score_key, capacity).astype(jnp.int32)
    busiest = jax.random.randint(owner_key, (), 0, N_DP)
    owners = jnp.arange(capacity, dtype=jnp.int32) // SLOTS
    scores = scores + jnp.where(owners == busiest, capacity, 0).astype(jnp.int32)
    order = jnp.argsort(-scores, stable=True)
    chosen = order[:BLOCKS]
    numbers = jax.random.permutation(block_key, BLOCKS).astype(jnp.int32)
    plan = jnp.full((capacity,), -1, jnp.int32).at[chosen].set(numbers)
    return plan.reshape(N_DP, SLOTS)


def draw_old_slots(key, part):
    key = jax.random.fold_in(key, 1)
    return owner_plan(key)


def draw_new_slots(key, part):
    key = jax.random.fold_in(key, 2)
    return owner_plan(key)


def placed_ranks(key, vector_shape):
    place_keys = jax.random.split(key, N_DP * SLOTS)
    ranks = jax.vmap(lambda one_key: jax.random.permutation(one_key, BLK))(place_keys)
    return ranks.reshape(vector_shape).astype(jnp.float32)


def kernel_of(positions, reach):
    distance = jnp.abs(positions[..., :, None] - positions[..., None, :])
    return jnp.exp(distance * (-1.0 / reach))


def draw_old_factors(key, part):
    plan = owner_plan(jax.random.fold_in(key, 1))
    key = jax.random.fold_in(key, 3)
    keys = jax.random.split(key, 8)
    place_key, jitter_key, diag_key, scale_key = (keys[0], keys[1], keys[2], keys[3])
    layer_key, second_key, second_jitter_key, block_key = (keys[4], keys[5], keys[6], keys[7])
    vector_shape = (N_DP, SLOTS, BLK)
    ranks = placed_ranks(place_key, vector_shape)
    second_ranks = placed_ranks(second_key, vector_shape)
    jitter = jax.random.uniform(jitter_key, vector_shape, jnp.float32, 0.0, 0.5)
    second_jitter = jax.random.uniform(second_jitter_key, vector_shape, jnp.float32, 0.0, 0.5)
    reach = BLK / 8.0
    diagonal = jnp.exp(jax.random.uniform(diag_key, vector_shape, jnp.float32, math.log(0.25), 0.0))
    scales = jnp.exp(jax.random.uniform(scale_key, vector_shape, jnp.float32, 0.0, math.log(3.2)))
    block_scale = jnp.exp(jax.random.uniform(block_key, (N_DP, SLOTS), jnp.float32, -math.log(3.0), math.log(3.0)))
    kernel = kernel_of(ranks + jitter, reach)
    second_kernel = kernel_of(second_ranks + second_jitter, BLK / 16.0)
    identity = jnp.eye(BLK, dtype=jnp.float32)
    matrix = kernel + 0.5 * second_kernel + diagonal[..., None] * identity
    matrix = matrix * scales[..., :, None] * scales[..., None, :]
    layer_scale = jnp.exp(jax.random.uniform(layer_key, (LAYERS,), jnp.float32, -math.log(10.0), math.log(10.0)))
    safe_ids = jnp.maximum(plan, 0)
    output_side = safe_ids % LAYER_BLOCKS >= A_SPAN
    slot_scale = jnp.where(output_side, layer_scale[safe_ids // LAYER_BLOCKS], 1.0) * block_scale
    return matrix * slot_scale[..., None, None]


def levels(key, extent, shards, smallest, high):
    loudness = 1.0
    for dim, shards_of in shards:
        steps = jax.random.uniform(jax.random.fold_in(jax.random.fold_in(key, 6), dim), (shards_of,), jnp.float32, smallest / len(shards), high / len(shards))
        loudness = loudness * jnp.repeat(jnp.exp(steps), extent[dim] // shards_of).reshape((-1,) + (1,) * (len(extent) - 1 - dim))
    return loudness


def gaussian(key, dims, deviation, bound, cuts=(), held_as=jnp.bfloat16):
    array = deviation * jax.random.normal(key, dims, jnp.float32)
    if cuts:
        array = array * levels(key, dims, cuts, -0.22, 0.18)
    return jnp.clip(array, -bound, bound).astype(held_as)


def setup_inputs(seed: int = 0) -> dict:
    arg_keys = jax.random.split(jax.random.key(seed), 5)
    old_factors = draw_old_factors(jax.random.fold_in(arg_keys[4], 71), 0)
    gradients = gaussian(arg_keys[1], (N_DP, TILES, ROWS_ALL, BLK), (2.0 / N_DP ** 0.5), 2.5, ((0, 128), (2, 4)))
    old_slots = draw_old_slots(jax.random.fold_in(arg_keys[4], 71), 0)
    new_slots = draw_new_slots(jax.random.fold_in(arg_keys[4], 71), 0)
    return dict(old_factors=old_factors, gradients=gradients, old_slots=old_slots, new_slots=new_slots)


damping_base = 2.0

def invert_block(packed):
    factor, shift_value = packed
    identity = jnp.eye(BLK, dtype=jnp.float32)
    lower_factor = jnp.linalg.cholesky(factor + shift_value * identity)
    lower_inverse = lax.linalg.triangular_solve(lower_factor, identity, left_side=True, lower=True)
    return jnp.dot(lower_inverse.T.astype(jnp.float32), lower_inverse.astype(jnp.float32), precision=lax.Precision.HIGHEST, preferred_element_type=jnp.float32)

def reference(old_factors, gradients, old_slots, new_slots):
    slot_total = N_DP * SLOTS
    block_ids = jnp.arange(BLOCKS, dtype=jnp.int32)
    layer_of = block_ids // LAYER_BLOCKS
    input_side = block_ids % LAYER_BLOCKS < A_SPAN
    slot_range = jnp.arange(slot_total, dtype=jnp.int32)
    flat_factors = old_factors.reshape(slot_total, BLK, BLK)
    old_flat = old_slots.reshape(slot_total)
    new_flat = new_slots.reshape(slot_total)
    old_place = lax.optimization_barrier(jnp.sum(jnp.where(old_flat[None, :] == block_ids[:, None], slot_range[None, :], 0), axis=1)).astype(jnp.int32)
    slot_traces = jnp.trace(flat_factors, axis1=1, axis2=2)
    block_traces = slot_traces[old_place]
    layer_ids = jnp.arange(LAYERS, dtype=jnp.int32)
    in_layer = layer_of[:, None] == layer_ids[None, :]
    trace_input = lax.optimization_barrier(jnp.sum(jnp.where(in_layer & input_side[:, None], block_traces[:, None], jnp.zeros((), jnp.float32)), axis=0))
    trace_output = lax.optimization_barrier(jnp.sum(jnp.where(in_layer & ~input_side[:, None], block_traces[:, None], jnp.zeros((), jnp.float32)), axis=0))
    trace_ratio = jnp.sqrt(trace_input / FF / (trace_output / D))
    block_ratio = trace_ratio[layer_of]
    shift_values = jnp.where(input_side, damping_base * block_ratio, damping_base / block_ratio)
    ordered = flat_factors[old_place]
    inverse_all = lax.map(invert_block, (ordered, shift_values)).astype(jnp.bfloat16)
    placed = jnp.where((new_flat >= 0)[:, None, None], inverse_all[jnp.maximum(new_flat, 0)], jnp.zeros((), jnp.bfloat16))
    inverses = placed.reshape(N_DP, SLOTS, BLK, BLK)

    def add_part(index, total):
        return total + gradients[index].astype(jnp.float32)
    gradient_total = lax.fori_loop(0, N_DP, add_part, jnp.zeros((TILES, ROWS_ALL, BLK), jnp.float32))
    gradient_sum = gradient_total.astype(jnp.bfloat16)
    tile_range = jnp.arange(TILES, dtype=jnp.int32)
    tile_block = tile_range // A_SPAN * LAYER_BLOCKS + tile_range % A_SPAN
    used = inverse_all[tile_block].astype(jnp.float32)
    product = jnp.einsum('wrk,wkj->wrj', gradient_sum.astype(jnp.float32), used, precision=lax.Precision.HIGHEST)
    return (inverses, product.astype(jnp.bfloat16))
```

```python
import jax
import jax.numpy as jnp
from jax import lax
from jax.experimental import pallas as pl
from jax.experimental.pallas import tpu as pltpu
from jax.sharding import Mesh, PartitionSpec as P

D = 8192
FF = 28672
DAMPING_BASE = 2.0
X_CORE = 8

BASE = 128
SUB = 8


def row_of(x, j):
    return jnp.broadcast_to(x[j : j + 1, :], x.shape)


def lane_of(x, j):
    return jnp.broadcast_to(x[:, j : j + 1], x.shape)


def base_sweep(load, store):
    groups = [load(i) for i in range(BASE // SUB)]
    sub_ids = lax.broadcasted_iota(jnp.int32, (SUB, BASE), 0)
    lane_ids = lax.broadcasted_iota(jnp.int32, (SUB, BASE), 1)
    for p in range(BASE // SUB):
        pivot_lanes = (lane_ids // SUB) == p
        spread = [lane_of(groups[p], p * SUB + j) for j in range(SUB)]
        unit = jnp.where(lane_ids == sub_ids + p * SUB, 1.0, 0.0)
        rows = jnp.where(pivot_lanes, unit, groups[p])
        for j in range(SUB):
            here = sub_ids == j
            scale = 1.0 / row_of(spread[j], j)
            line = row_of(rows, j) * scale
            rows = jnp.where(here, line, rows - spread[j] * line)
            for i in range(j + 1, SUB):
                part = row_of(spread[i], j) * scale
                spread[i] = jnp.where(here, part, spread[i] - spread[j] * part)
        rows = jnp.where(pivot_lanes, -rows, rows)
        lines = [row_of(rows, j) for j in range(SUB)]
        for i in range(BASE // SUB):
            if i == p:
                continue
            total = jnp.where(pivot_lanes, 0.0, groups[i])
            for j in range(SUB):
                total = total - lane_of(groups[i], p * SUB + j) * lines[j]
            groups[i] = total
        groups[p] = rows
    for i in range(BASE // SUB):
        store(i, groups[i])


def halves(x):
    high = x.astype(jnp.bfloat16)
    return high, (x - high.astype(jnp.float32)).astype(jnp.bfloat16)


def dot3(left, right):
    def one(a, b):
        return jnp.dot(a, b, preferred_element_type=jnp.float32)

    return one(left[0], right[0]) + (one(left[0], right[1]) + one(left[1], right[0]))


def invert_kernel(
    scalar_ref, shift_ref, rows_ref, one_ref, two_ref, three_ref,
    band_ref, full_ref, m_ref, d_ref, th_ref, tl_ref,
):
    n = rows_ref.shape[1]
    wide = rows_ref.shape[0]
    count = n // wide
    mp_index = scalar_ref[1]

    def block(i):
        return slice(i * wide, (i + 1) * wide)

    def place(i):
        return pl.ds(pl.multiple_of(lax.rem(mp_index + i, count) * wide, wide), wide)

    @pl.when(scalar_ref[0] > 0)
    def _():
        eye = jnp.where(
            lax.broadcasted_iota(jnp.int32, (wide, wide), 0)
            == lax.broadcasted_iota(jnp.int32, (wide, wide), 1),
            shift_ref[0],
            0.0,
        )

        def put(i, j, value):
            if i == j:
                m_ref[block(i), block(i)] = value + eye
            else:
                m_ref[block(i), block(j)] = value
                m_ref[block(j), block(i)] = value.T

        for j in range(count):
            put(0, j, rows_ref[:, place(j)])
        put(1, 1, one_ref[:, block(0)])
        put(1, 2, one_ref[:, block(1)])
        put(2, 2, two_ref[:, block(0)])
        put(2, 3, two_ref[:, block(1)])
        put(3, 3, three_ref[:, block(0)])
        put(3, 1, three_ref[:, block(1)])

        @pl.loop(0, count)
        def _(k):
            at = pl.ds(pl.multiple_of(k * wide, wide), wide)

            d_ref[...] = m_ref[at, at]

            def sweep_half(h):
                lo = h * BASE
                base_sweep(
                    lambda i: d_ref[lo + i * SUB : lo + (i + 1) * SUB, lo : lo + BASE],
                    lambda i, v: d_ref.__setitem__(
                        (slice(lo + i * SUB, lo + (i + 1) * SUB), slice(lo, lo + BASE)), v
                    ),
                )

            one, two = slice(0, BASE), slice(BASE, wide)
            sweep_half(0)
            minus_p = halves(d_ref[one, one])
            cross = halves(d_ref[one, two])
            cross_t = halves(d_ref[two, one])
            t_halves = halves(-dot3(minus_p, cross))
            d_ref[two, two] = d_ref[two, two] - dot3(cross_t, t_halves)
            left = halves(-dot3(cross_t, minus_p))
            sweep_half(1)
            minus_p = halves(d_ref[two, two])
            up = dot3(t_halves, minus_p)
            d_ref[one, one] = d_ref[one, one] + dot3(halves(up), left)
            d_ref[one, two] = -up
            d_ref[two, one] = -dot3(minus_p, left)

            minus_p = halves(d_ref[...])
            col_h, col_l = halves(m_ref[:, at])
            rows = -dot3(minus_p, halves(m_ref[at, :]))
            m_ref[:, at] = jnp.zeros((n, wide), jnp.float32)
            m_ref[at, :] = rows
            m_ref[at, at] = d_ref[...]
            th_ref[...], tl_ref[...] = halves(m_ref[at, :])
            for i in range(count):

                @pl.when(i != k)
                def _():
                    m_ref[block(i), :] = m_ref[block(i), :] - dot3(
                        (col_h[block(i)], col_l[block(i)]), (th_ref[...], tl_ref[...])
                    )

        for j in range(count):
            band_ref[:, place(j)] = (-m_ref[block(0), block(j)]).astype(jnp.bfloat16)
            for i in range(count):
                full_ref[place(i), place(j)] = (-m_ref[block(i), block(j)]).astype(jnp.bfloat16)

    @pl.when(scalar_ref[0] <= 0)
    def _():
        band_ref[...] = jnp.zeros(band_ref.shape, jnp.bfloat16)
        full_ref[...] = jnp.zeros(full_ref.shape, jnp.bfloat16)


def invert(scalars, shift, rows, one, two, three):
    wide, n = rows.shape
    in_smem = pl.BlockSpec(memory_space=pltpu.SMEM)
    in_vmem = pl.BlockSpec(memory_space=pltpu.VMEM)
    return pl.pallas_call(
        invert_kernel,
        out_shape=(
            jax.ShapeDtypeStruct((wide, n), jnp.bfloat16),
            jax.ShapeDtypeStruct((n, n), jnp.bfloat16),
        ),
        in_specs=[in_smem] * 2 + [in_vmem] * 4,
        out_specs=(in_vmem, in_vmem),
        scratch_shapes=[
            pltpu.VMEM((n, n), jnp.float32),
            pltpu.VMEM((wide, wide), jnp.float32),
            pltpu.VMEM((wide, n), jnp.bfloat16),
            pltpu.VMEM((wide, n), jnp.bfloat16),
        ],
        compiler_params=pltpu.CompilerParams(vmem_limit_bytes=40 * 1024 * 1024),
        cost_estimate=pl.CostEstimate(
            flops=48 * n * n * n, bytes_accessed=6 * n * n, transcendentals=0
        ),
    )(scalars, shift, rows, one, two, three)


def positions(slot_ids, wanted):
    slot_range = jnp.arange(slot_ids.shape[0], dtype=jnp.int32)
    hit = slot_ids[None, :] == wanted[:, None]
    return jnp.sum(jnp.where(hit, slot_range[None, :], 0), axis=1).astype(jnp.int32)


def exchange(pieces, axes):
    return lax.all_to_all(pieces, axes, split_axis=0, concat_axis=0, tiled=True)


def from_all(piece, axes, count):
    return exchange(jnp.broadcast_to(piece[None], (count,) + piece.shape), axes)


DP = ("z", "xc")


def local(old_factors, gradients, old_slots, new_slots):
    mp_index = lax.axis_index("mp")
    mp_count = lax.axis_size("mp")
    z_count, xc_count = lax.axis_size("z"), lax.axis_size("xc")
    dp_count = z_count * xc_count
    dp_index = lax.axis_index("z") * xc_count + lax.axis_index("xc")
    band, width = old_factors.shape[2:]
    tile_count, row_count = gradients.shape[1:3]
    a_span = FF // width
    layer_blocks = a_span + D // width
    layers = tile_count // a_span
    old_flat = old_slots.reshape(dp_count)
    new_flat = new_slots.reshape(dp_count)

    rows = old_factors[0, 0]
    doubled = jnp.concatenate([rows, rows], axis=1)
    ahead = lax.dynamic_slice_in_dim(doubled, mp_index * band, 3 * band, 1)
    near = ahead[:, : 2 * band]
    far = jnp.concatenate([ahead[:, :band], ahead[:, 2 * band :]], axis=1)

    def from_next(value, step):
        return lax.ppermute(
            value, "mp", [((i + step) % mp_count, i) for i in range(mp_count)]
        )

    one = from_next(near, 1)
    two = from_next(near, 2)
    three = from_next(far, 3)

    trace = jnp.trace(ahead[:, :band])
    lanes = jnp.full((1, 128), trace, jnp.float32)
    block_trace = jnp.sum(from_all(lanes, "mp", mp_count), axis=0)
    slot_traces = from_all(block_trace, DP, dp_count)[:, 0, 0]
    layer_ids = jnp.arange(layers, dtype=jnp.int32)
    held = old_flat >= 0
    slot_input = old_flat % layer_blocks < a_span
    in_layer = held[None, :] & (old_flat[None, :] // layer_blocks == layer_ids[:, None])
    trace_input = jnp.sum(jnp.where(in_layer & slot_input[None, :], slot_traces[None, :], 0.0), axis=1)
    trace_output = jnp.sum(jnp.where(in_layer & ~slot_input[None, :], slot_traces[None, :], 0.0), axis=1)
    ratios = jnp.sqrt(trace_input / FF / (trace_output / D))
    own = lax.dynamic_index_in_dim(old_flat, dp_index, keepdims=False)
    own_block = jnp.maximum(own, 0)
    own_layer = own_block // layer_blocks
    own_input = own_block % layer_blocks < a_span
    ratio = jnp.sum(jnp.where(layer_ids == own_layer, ratios, 0.0))
    shift = jnp.where(own_input, DAMPING_BASE * ratio, DAMPING_BASE / ratio)

    lane = 128
    parts = gradients[0].reshape(2, tile_count // 2, row_count, width // lane, lane)
    parts = parts.transpose(0, 2, 3, 1, 4).reshape(dp_count, tile_count // 2, lane)
    parts = exchange(parts, DP)

    scalars = jnp.stack([(own >= 0).astype(jnp.int32), mp_index.astype(jnp.int32)])
    inverse_band, inverse = invert(scalars, shift.reshape(1), rows, one, two, three)

    spread = exchange(inverse_band.reshape(dp_count, band // dp_count, width), DP)
    slot_range = jnp.arange(dp_count, dtype=jnp.int32)
    empty = jnp.min(jnp.where(held, dp_count - 1, slot_range))
    source = jnp.where(new_flat >= 0, positions(old_flat, new_flat), empty)
    arrived = exchange(jnp.take(spread, source, axis=0), DP)
    inverses = arrived.reshape(1, 1, band, width)

    summed = jnp.sum(parts.astype(jnp.float32), axis=0).astype(jnp.bfloat16).astype(jnp.float32)
    block = jnp.maximum(old_flat, 0)
    tile_of = jnp.minimum(block // layer_blocks * a_span + block % layer_blocks, tile_count - 1)
    half_tiles = tile_count // 2
    tile_rows = jnp.take(summed, tile_of % half_tiles, axis=0)
    tile_rows = exchange(tile_rows.reshape(dp_count, 1, lane), DP)
    own_tile = jnp.minimum(own_layer * a_span + own_block % layer_blocks, tile_count - 1)
    tile_rows = lax.dynamic_slice_in_dim(
        tile_rows, own_tile // half_tiles * (dp_count // 2), dp_count // 2, 0
    )
    tile = tile_rows.reshape(row_count, width).astype(jnp.bfloat16)
    result = jnp.dot(tile, inverse, preferred_element_type=jnp.float32).astype(jnp.bfloat16)
    gathered = from_all(from_all(result, "z", z_count), "xc", xc_count)
    gathered = gathered.reshape(dp_count, row_count, width)
    tile_range = jnp.arange(tile_count, dtype=jnp.int32)
    place = positions(old_flat, tile_range // a_span * layer_blocks + tile_range % a_span)
    precond = jnp.take(gathered, place % xc_count * z_count + place // xc_count, axis=0)
    return (inverses, precond)


def solution(mesh):
    dp_count, mp_count = mesh.devices.shape
    parts = Mesh(
        mesh.devices.reshape(dp_count // X_CORE, X_CORE, mp_count), ("z", "xc", "mp")
    )
    in_specs = (P(DP, None, "mp", None), P(DP, None, "mp", None), P(), P())
    out_specs = (P(DP, None, "mp", None), P(None, "mp", None))
    return jax.shard_map(local, mesh=parts, in_specs=in_specs, out_specs=out_specs, check_vma=False)
```

```python
import jax
import jax.numpy as jnp
from jax import lax
from jax.experimental import pallas as pl
from jax.experimental.pallas import tpu as pltpu
from jax.sharding import Mesh, PartitionSpec as P

D = 8192
FF = 28672
DAMPING_BASE = 2.0
X_COUNT, CORES = 4, 2
DP = ("z", "x", "c")

BASE = 128
SUB = 8
ROWS, LANES = 16, 128


def row_of(x, j):
    return jnp.broadcast_to(x[j : j + 1, :], x.shape)


def lane_of(x, j):
    return jnp.broadcast_to(x[:, j : j + 1], x.shape)


def reciprocal(x):
    return pltpu.reciprocal(x, approx=True)


def base_sweep(load, store):
    count = BASE // SUB
    groups = [load(i) for i in range(count)]
    sub_ids = lax.broadcasted_iota(jnp.int32, (SUB, BASE), 0)
    lane_ids = lax.broadcasted_iota(jnp.int32, (SUB, BASE), 1)
    for p in range(count):
        pivot_lanes = (lane_ids // SUB) == p
        spread = [lane_of(groups[p], p * SUB + j) for j in range(SUB)]
        rows = jnp.where(pivot_lanes, jnp.where(lane_ids == sub_ids + p * SUB, 1.0, 0.0), groups[p])
        pivot = row_of(spread[0], 0)
        for j in range(SUB):
            here = sub_ids == j
            scale = reciprocal(pivot)
            if j + 1 < SUB:
                cross = row_of(spread[j], j + 1) * row_of(spread[j + 1], j)
                pivot = row_of(spread[j + 1], j + 1) - cross * scale
            column = jnp.where(here, -1.0, spread[j])

            def eliminate(x):
                line = row_of(x, j)
                return jnp.where(here, 0.0, x) - (column * line) * scale

            rows = eliminate(rows)
            for i in range(j + 1, SUB):
                spread[i] = eliminate(spread[i])
        rows = jnp.where(pivot_lanes, -rows, rows)
        lines = [row_of(rows, j) for j in range(SUB)]
        for step in range(1, count):
            i = (p + step) % count
            terms = [lane_of(groups[i], p * SUB + j) * lines[j] for j in range(SUB)]
            while len(terms) > 1:
                terms = [a + b for a, b in zip(terms[::2], terms[1::2])]
            groups[i] = jnp.where(pivot_lanes, 0.0, groups[i]) - terms[0]
        groups[p] = rows
    for i in range(count):
        store(i, groups[i])


def halves(x):
    high = x.astype(jnp.bfloat16)
    return high, (x - high.astype(jnp.float32)).astype(jnp.bfloat16)


def dot3(left, right):
    def one(a, b):
        return jnp.dot(a, b, preferred_element_type=jnp.float32)

    return one(left[0], right[0]) + (one(left[0], right[1]) + one(left[1], right[0]))


def invert_kernel(
    scalar_ref, shift_ref, rows_ref, one_ref, two_ref, three_ref,
    band_ref, full_ref, m_ref, d_ref, th_ref, tl_ref,
):
    n = rows_ref.shape[1]
    wide = rows_ref.shape[0]
    count = n // wide
    mp_index = scalar_ref[1]

    def block(i):
        return slice(i * wide, (i + 1) * wide)

    def place(i):
        return pl.ds(pl.multiple_of(lax.rem(mp_index + i, count) * wide, wide), wide)

    @pl.when(scalar_ref[0] > 0)
    def _():
        eye = jnp.where(
            lax.broadcasted_iota(jnp.int32, (wide, wide), 0)
            == lax.broadcasted_iota(jnp.int32, (wide, wide), 1),
            shift_ref[0],
            0.0,
        )

        def put(i, j, value):
            if i == j:
                m_ref[block(i), block(i)] = value + eye
            else:
                m_ref[block(i), block(j)] = value
                m_ref[block(j), block(i)] = value.T

        for j in range(count):
            put(0, j, rows_ref[:, place(j)])
        put(1, 1, one_ref[:, block(0)])
        put(1, 2, one_ref[:, block(1)])
        put(2, 2, two_ref[:, block(0)])
        put(2, 3, two_ref[:, block(1)])
        put(3, 3, three_ref[:, block(0)])
        put(3, 1, three_ref[:, block(1)])

        @pl.loop(0, count)
        def _(k):
            at = pl.ds(pl.multiple_of(k * wide, wide), wide)

            d_ref[...] = m_ref[at, at]

            def sweep_half(h):
                lo = h * BASE
                base_sweep(
                    lambda i: d_ref[lo + i * SUB : lo + (i + 1) * SUB, lo : lo + BASE],
                    lambda i, v: d_ref.__setitem__(
                        (slice(lo + i * SUB, lo + (i + 1) * SUB), slice(lo, lo + BASE)), v
                    ),
                )

            one, two = slice(0, BASE), slice(BASE, wide)
            sweep_half(0)
            minus_p = halves(d_ref[one, one])
            cross = halves(d_ref[one, two])
            cross_t = halves(d_ref[two, one])
            t_halves = halves(-dot3(minus_p, cross))
            d_ref[two, two] = d_ref[two, two] - dot3(cross_t, t_halves)
            left = halves(-dot3(cross_t, minus_p))
            sweep_half(1)
            minus_p = halves(d_ref[two, two])
            up = dot3(t_halves, minus_p)
            d_ref[one, one] = d_ref[one, one] + dot3(halves(up), left)
            d_ref[one, two] = -up
            d_ref[two, one] = -dot3(minus_p, left)

            minus_p = halves(d_ref[...])
            col_h, col_l = halves(m_ref[:, at])
            rows = -dot3(minus_p, halves(m_ref[at, :]))
            m_ref[:, at] = jnp.zeros((n, wide), jnp.float32)
            m_ref[at, :] = rows
            m_ref[at, at] = d_ref[...]
            th_ref[...], tl_ref[...] = halves(m_ref[at, :])
            for i in range(count):

                @pl.when(i != k)
                def _():
                    m_ref[block(i), :] = m_ref[block(i), :] - dot3(
                        (col_h[block(i)], col_l[block(i)]), (th_ref[...], tl_ref[...])
                    )

        for j in range(count):
            band = (-m_ref[block(0), block(j)]).astype(jnp.bfloat16)
            for r in range(wide // ROWS):
                for c in range(wide // LANES):
                    at = lax.rem(mp_index + j, count) * (wide // LANES) + r * (n // LANES) + c
                    band_ref[at] = band[r * ROWS : (r + 1) * ROWS, c * LANES : (c + 1) * LANES]
            for i in range(count):
                full_ref[place(i), place(j)] = (-m_ref[block(i), block(j)]).astype(jnp.bfloat16)

    @pl.when(scalar_ref[0] <= 0)
    def _():
        band_ref[...] = jnp.zeros(band_ref.shape, jnp.bfloat16)
        full_ref[...] = jnp.zeros(full_ref.shape, jnp.bfloat16)


def invert(scalars, shift, rows, one, two, three):
    wide, n = rows.shape
    in_smem = pl.BlockSpec(memory_space=pltpu.SMEM)
    in_vmem = pl.BlockSpec(memory_space=pltpu.VMEM)
    return pl.pallas_call(
        invert_kernel,
        out_shape=(
            jax.ShapeDtypeStruct((wide * n // (ROWS * LANES), ROWS, LANES), jnp.bfloat16),
            jax.ShapeDtypeStruct((n, n), jnp.bfloat16),
        ),
        in_specs=[in_smem] * 2 + [in_vmem] * 4,
        out_specs=(in_vmem, in_vmem),
        scratch_shapes=[
            pltpu.VMEM((n, n), jnp.float32),
            pltpu.VMEM((wide, wide), jnp.float32),
            pltpu.VMEM((wide, n), jnp.bfloat16),
            pltpu.VMEM((wide, n), jnp.bfloat16),
        ],
        compiler_params=pltpu.CompilerParams(vmem_limit_bytes=24 * 1024 * 1024),
        cost_estimate=pl.CostEstimate(
            flops=36 * n * n * n, bytes_accessed=6 * n * n, transcendentals=0
        ),
    )(scalars, shift, rows, one, two, three)


def pick_kernel(index_ref, src_ref, out_ref):
    @pl.loop(0, out_ref.shape[0], unroll=8)
    def _(i):
        out_ref[i] = src_ref[index_ref[i]]


def pick(index, source):
    in_vmem = pl.BlockSpec(memory_space=pltpu.VMEM)
    return pl.pallas_call(
        pick_kernel,
        out_shape=jax.ShapeDtypeStruct(index.shape + source.shape[1:], source.dtype),
        in_specs=[pl.BlockSpec(memory_space=pltpu.SMEM), in_vmem],
        out_specs=in_vmem,
        compiler_params=pltpu.CompilerParams(vmem_limit_bytes=4 * 1024 * 1024),
    )(index, source)


def take(source, index):
    return source.at[index].get(mode="promise_in_bounds")


def positions(slot_ids, wanted):
    slot_range = jnp.arange(slot_ids.shape[0], dtype=jnp.int32)
    hit = slot_ids[None, :] == wanted[:, None]
    return jnp.sum(jnp.where(hit, slot_range[None, :], 0), axis=1).astype(jnp.int32)


def exchange(pieces, axes):
    return lax.all_to_all(pieces, axes, split_axis=0, concat_axis=0, tiled=True)


def from_ahead(value, axis, step):
    count = lax.axis_size(axis)
    return lax.ppermute(value, axis, [((i + step) % count, i) for i in range(count)])


def sum_of_all(value, axes, count):
    return jnp.sum(exchange(jnp.broadcast_to(value[None], (count,) + value.shape), axes), axis=0)


def local(old_factors, gradients, old_slots, new_slots):
    mp_index = lax.axis_index("mp")
    mp_count = lax.axis_size("mp")
    z_count, x_count, c_count = lax.axis_size("z"), lax.axis_size("x"), lax.axis_size("c")
    z, x, c = lax.axis_index("z"), lax.axis_index("x"), lax.axis_index("c")
    dp_count = z_count * x_count * c_count
    dp_index = (z * x_count + x) * c_count + c
    band, width = old_factors.shape[2:]
    tile_count, row_count = gradients.shape[1:3]
    a_span = FF // width
    layer_blocks = a_span + D // width
    layers = tile_count // a_span
    old_flat = old_slots.reshape(dp_count)
    new_flat = new_slots.reshape(dp_count)
    own = lax.dynamic_index_in_dim(old_flat, dp_index, keepdims=False)
    own_block = jnp.maximum(own, 0)
    own_layer = own_block // layer_blocks
    own_input = own_block % layer_blocks < a_span

    rows = old_factors[0, 0]
    trace = jnp.trace(lax.dynamic_slice_in_dim(rows, mp_index * band, band, 1))
    bins = lax.broadcasted_iota(jnp.int32, (1, 128), 1)
    own_bin = jnp.where(own >= 0, 2 * own_layer + jnp.where(own_input, 0, 1), -1)
    binned = jnp.where(bins == own_bin, trace, 0.0)
    binned = sum_of_all(binned, ("x", "c", "mp"), x_count * c_count * mp_count)
    binned = sum_of_all(binned, "z", z_count)
    trace_input = jnp.sum(jnp.where(bins == 2 * own_layer, binned, 0.0))
    trace_output = jnp.sum(jnp.where(bins == 2 * own_layer + 1, binned, 0.0))
    ratio = jnp.sqrt(trace_input / FF / (trace_output / D))
    shift = jnp.where(own_input, DAMPING_BASE * ratio, DAMPING_BASE / ratio)

    doubled = jnp.concatenate([rows, rows], axis=1)
    ahead = lax.dynamic_slice_in_dim(doubled, mp_index * band, 3 * band, 1)
    near = ahead[:, : 2 * band]
    far = jnp.concatenate([ahead[:, :band], ahead[:, 2 * band :]], axis=1)
    one = from_ahead(near, "mp", 1)
    two = from_ahead(near, "mp", 2)
    three = from_ahead(far, "mp", 3)

    block = jnp.maximum(old_flat, 0)
    tile_of = jnp.minimum(block // layer_blocks * a_span + block % layer_blocks, tile_count - 1)
    tile_of = tile_of.reshape(z_count, x_count, c_count).transpose(2, 1, 0)

    def tiles_of(core):
        index = lax.dynamic_index_in_dim(tile_of, core, keepdims=False)
        return take(gradients[0], index.reshape(-1))

    def split(value):
        return value.astype(jnp.float32).reshape(x_count, z_count, row_count, width)

    arrived = from_ahead(tiles_of(1 - c), "c", 1)
    partial = split(tiles_of(c)) + split(arrived)
    total = lax.dynamic_index_in_dim(partial, x, keepdims=False)
    for step in range(1, x_count):
        piece = lax.dynamic_index_in_dim(partial, (x + x_count - step) % x_count, keepdims=False)
        total = total + from_ahead(piece, "x", step)
    shift, total = lax.optimization_barrier((shift, total))
    tile = jnp.sum(exchange(total, "z"), axis=0).astype(jnp.bfloat16)

    scalars = jnp.stack([(own >= 0).astype(jnp.int32), mp_index.astype(jnp.int32)])
    inverse_band, inverse = invert(scalars, shift.reshape(1), rows, one, two, three)
    inverse_band, tile = lax.optimization_barrier((inverse_band, tile))

    spread = exchange(inverse_band, DP)
    slot_range = jnp.arange(dp_count, dtype=jnp.int32)
    empty = jnp.min(jnp.where(old_flat >= 0, dp_count - 1, slot_range))
    source = jnp.where(new_flat >= 0, positions(old_flat, new_flat), empty)
    arrived = exchange(pick(source, spread), DP)
    arrived = arrived.reshape(band // ROWS, width // LANES, ROWS, LANES)
    inverses = arrived.transpose(0, 2, 1, 3).reshape(1, 1, band, width)

    held = jnp.dot(tile, inverse, preferred_element_type=jnp.float32).astype(jnp.bfloat16)
    for axis, steps in (("z", (4, 8, 12)), ("z", (1, 2, 15)), ("x", (1, 2, 3)), ("c", (1,))):
        held = jnp.stack([held] + [from_ahead(held, axis, step) for step in steps])
    held = held.reshape(dp_count, row_count, width)
    tile_range = jnp.arange(tile_count, dtype=jnp.int32)
    place = positions(old_flat, tile_range // a_span * layer_blocks + tile_range % a_span)
    far_z = (place // (x_count * c_count) - z + z_count) % z_count
    far_x = (place // c_count - x + x_count) % x_count
    far_c = (place - c + c_count) % c_count
    low = far_z % 4
    high = (far_z + jnp.where(low == 3, 1, 0)) // 4 % 4
    precond = take(held, ((far_c * x_count + far_x) * 4 + low) * 4 + high)
    return (inverses, precond)


def solution(mesh):
    dp_count, mp_count = mesh.devices.shape
    z_count = dp_count // (X_COUNT * CORES)
    parts = Mesh(
        mesh.devices.reshape(z_count, X_COUNT, CORES, mp_count), DP + ("mp",)
    )
    in_specs = (P(DP, None, "mp", None), P(DP, None, "mp", None), P(), P())
    out_specs = (P(DP, None, "mp", None), P(None, "mp", None))
    return jax.shard_map(local, mesh=parts, in_specs=in_specs, out_specs=out_specs, check_vma=False)
```

```python
import jax
import jax.numpy as jnp
from jax import lax
from jax.experimental import pallas as pl
from jax.experimental.pallas import tpu as pltpu
from jax.sharding import Mesh, PartitionSpec as P

D = 8192
FF = 28672
DAMPING_BASE = 2.0
X_COUNT, CORES = 4, 2
DP = ("z", "x", "c")

BASE = 32
SUB = 8
ROWS, LANES = 16, 128


def row_of(x, j):
    return jnp.broadcast_to(x[j : j + 1, :], x.shape)


def lane_of(x, j):
    return jnp.broadcast_to(x[:, j : j + 1], x.shape)


def reciprocal(x):
    return pltpu.reciprocal(x, approx=True)


def halves(x):
    high = x.astype(jnp.bfloat16)
    return high, (x - high.astype(jnp.float32)).astype(jnp.bfloat16)


def stacked(x, order, axis):
    parts = halves(x)
    return jnp.concatenate([parts[i] for i in order], axis=axis)


LEFT, RIGHT = (0, 0, 1), (0, 1, 0)


def dot(left, right):
    return jnp.dot(left, right, preferred_element_type=jnp.float32)


def panel_sweep(groups, first):
    sub_ids = lax.broadcasted_iota(jnp.int32, (SUB, LANES), 0)
    lane_ids = lax.broadcasted_iota(jnp.int32, (SUB, LANES), 1)
    for p in range(len(groups)):
        tile, lane = divmod(first + p * SUB, LANES)
        pivot_lanes = (lane_ids // SUB) == lane // SUB
        spread = [lane_of(groups[p][tile], lane + j) for j in range(SUB)]
        rows = list(groups[p])
        rows[tile] = jnp.where(
            pivot_lanes, jnp.where(lane_ids == sub_ids + lane, 1.0, 0.0), rows[tile]
        )
        pivot = row_of(spread[0], 0)
        for j in range(SUB):
            here = sub_ids == j
            scale = reciprocal(pivot)
            if j + 1 < SUB:
                cross = row_of(spread[j], j + 1) * row_of(spread[j + 1], j)
                pivot = row_of(spread[j + 1], j + 1) - cross * scale
            column = jnp.where(here, -1.0, spread[j])

            def eliminate(x):
                line = row_of(x, j)
                return jnp.where(here, 0.0, x) - (column * line) * scale

            rows = [eliminate(x) for x in rows]
            for i in range(j + 1, SUB):
                spread[i] = eliminate(spread[i])
        rows[tile] = jnp.where(pivot_lanes, -rows[tile], rows[tile])
        lines = [[row_of(x, j) for x in rows] for j in range(SUB)]
        for g in range(len(groups)):
            if g == p:
                continue
            factors = [lane_of(groups[g][tile], lane + j) for j in range(SUB)]
            for t in range(len(rows)):
                terms = [factors[j] * lines[j][t] for j in range(SUB)]
                while len(terms) > 1:
                    terms = [a + b for a, b in zip(terms[::2], terms[1::2])]
                kept = groups[g][t]
                if t == tile:
                    kept = jnp.where(pivot_lanes, 0.0, kept)
                groups[g][t] = kept - terms[0]
        groups[p] = rows
    return groups


def block_sweep(d_ref):
    wide = d_ref.shape[0]
    lane_ids = lax.broadcasted_iota(jnp.int32, (wide, wide), 1)
    for first in range(0, wide, BASE):
        old = d_ref[first : first + BASE, :]
        groups = [
            [old[g : g + SUB, t : t + LANES] for t in range(0, wide, LANES)]
            for g in range(0, BASE, SUB)
        ]
        groups = panel_sweep(groups, first)
        new = jnp.concatenate([jnp.concatenate(g, axis=1) for g in groups], axis=0)
        update = lax.dot_general(
            stacked(old, LEFT, 0),
            stacked(new, RIGHT, 0),
            (((0,), (0,)), ((), ())),
            preferred_element_type=jnp.float32,
        )
        kept = jnp.where(lane_ids // BASE == first // BASE, 0.0, d_ref[...])
        d_ref[...] = kept - update
        d_ref[first : first + BASE, :] = new


def invert_kernel(
    scalar_ref, shift_ref, rows_ref, one_hbm, two_hbm, three_hbm,
    band_ref, full_ref, m_ref, d_ref, left_ref, right_ref, far_ref, far_sem,
):
    n = rows_ref.shape[1]
    wide = rows_ref.shape[0]
    count = n // wide
    mp_index = scalar_ref[1]

    def block(i):
        return slice(i * wide, (i + 1) * wide)

    def place(i):
        return pl.ds(pl.multiple_of(lax.rem(mp_index + i, count) * wide, wide), wide)

    @pl.when(scalar_ref[0] > 0)
    def _():
        copies = [
            pltpu.make_async_copy(source, far_ref.at[i], far_sem.at[i])
            for i, source in enumerate((one_hbm, two_hbm, three_hbm))
        ]
        for copy in copies:
            copy.start()
        eye = jnp.where(
            lax.broadcasted_iota(jnp.int32, (wide, wide), 0)
            == lax.broadcasted_iota(jnp.int32, (wide, wide), 1),
            shift_ref[0],
            0.0,
        )

        def put(i, j, value):
            if i == j:
                m_ref[block(i), block(i)] = value + eye
            else:
                m_ref[block(i), block(j)] = value
                m_ref[block(j), block(i)] = value.T

        for j in range(count):
            put(0, j, rows_ref[:, place(j)])
        for i in range(1, count):
            copies[i - 1].wait()
            put(i, i, far_ref[i - 1, :, block(0)])
            put(i, i % (count - 1) + 1, far_ref[i - 1, :, block(1)])

        @pl.loop(0, count)
        def _(k):
            at = pl.ds(pl.multiple_of(k * wide, wide), wide)
            d_ref[...] = m_ref[at, at]
            block_sweep(d_ref)

            left_ref[...] = stacked(m_ref[:, at], LEFT, 1)
            right_ref[...] = stacked(m_ref[at, :], RIGHT, 0)
            rows = -dot(stacked(d_ref[...], LEFT, 1), right_ref[...])
            m_ref[:, at] = jnp.zeros((n, wide), jnp.float32)
            m_ref[at, :] = rows
            m_ref[at, at] = d_ref[...]
            right_ref[...] = stacked(m_ref[at, :], RIGHT, 0)
            for i in range(count):

                @pl.when(i != k)
                def _():
                    m_ref[block(i), :] = m_ref[block(i), :] - dot(left_ref[block(i), :], right_ref[...])

        for j in range(count):
            band = (-m_ref[block(0), block(j)]).astype(jnp.bfloat16)
            for r in range(wide // ROWS):
                for c in range(wide // LANES):
                    at = lax.rem(mp_index + j, count) * (wide // LANES) + r * (n // LANES) + c
                    band_ref[at] = band[r * ROWS : (r + 1) * ROWS, c * LANES : (c + 1) * LANES]
            for i in range(count):
                full_ref[place(i), place(j)] = (-m_ref[block(i), block(j)]).astype(jnp.bfloat16)

    @pl.when(scalar_ref[0] <= 0)
    def _():
        band_ref[...] = jnp.zeros(band_ref.shape, jnp.bfloat16)
        full_ref[...] = jnp.zeros(full_ref.shape, jnp.bfloat16)


def invert(scalars, shift, rows, one, two, three):
    wide, n = rows.shape
    in_smem = pl.BlockSpec(memory_space=pltpu.SMEM)
    in_vmem = pl.BlockSpec(memory_space=pltpu.VMEM)
    anywhere = pl.BlockSpec(memory_space=pl.ANY)
    return pl.pallas_call(
        invert_kernel,
        out_shape=(
            jax.ShapeDtypeStruct((wide * n // (ROWS * LANES), ROWS, LANES), jnp.bfloat16),
            jax.ShapeDtypeStruct((n, n), jnp.bfloat16),
        ),
        in_specs=[in_smem] * 2 + [in_vmem] + [anywhere] * 3,
        out_specs=(in_vmem, in_vmem),
        scratch_shapes=[
            pltpu.VMEM((n, n), jnp.float32),
            pltpu.VMEM((wide, wide), jnp.float32),
            pltpu.VMEM((n, 3 * wide), jnp.bfloat16),
            pltpu.VMEM((3 * wide, n), jnp.bfloat16),
            pltpu.VMEM((3, wide, 2 * wide), jnp.float32),
            pltpu.SemaphoreType.DMA((3,)),
        ],
        compiler_params=pltpu.CompilerParams(vmem_limit_bytes=24 * 1024 * 1024),
        cost_estimate=pl.CostEstimate(
            flops=36 * n * n * n, bytes_accessed=6 * n * n, transcendentals=0
        ),
    )(scalars, shift, rows, one, two, three)


def pick_kernel(index_ref, src_ref, out_ref):
    @pl.loop(0, out_ref.shape[0], unroll=8)
    def _(i):
        out_ref[i] = src_ref[index_ref[i]]


def pick(index, source):
    in_vmem = pl.BlockSpec(memory_space=pltpu.VMEM)
    return pl.pallas_call(
        pick_kernel,
        out_shape=jax.ShapeDtypeStruct(index.shape + source.shape[1:], source.dtype),
        in_specs=[pl.BlockSpec(memory_space=pltpu.SMEM), in_vmem],
        out_specs=in_vmem,
        compiler_params=pltpu.CompilerParams(vmem_limit_bytes=4 * 1024 * 1024),
    )(index, source)


def take(source, index):
    return source.at[index].get(mode="promise_in_bounds")


def positions(slot_ids, wanted):
    slot_range = jnp.arange(slot_ids.shape[0], dtype=jnp.int32)
    hit = slot_ids[None, :] == wanted[:, None]
    return jnp.sum(jnp.where(hit, slot_range[None, :], 0), axis=1).astype(jnp.int32)


def exchange(pieces, axes):
    return lax.all_to_all(pieces, axes, split_axis=0, concat_axis=0, tiled=True)


def from_ahead(value, axis, step):
    count = lax.axis_size(axis)
    return lax.ppermute(value, axis, [((i + step) % count, i) for i in range(count)])


def sum_of_all(value, axes, count):
    return jnp.sum(exchange(jnp.broadcast_to(value[None], (count,) + value.shape), axes), axis=0)


def local(old_factors, gradients, old_slots, new_slots):
    mp_index = lax.axis_index("mp")
    mp_count = lax.axis_size("mp")
    z_count, x_count, c_count = lax.axis_size("z"), lax.axis_size("x"), lax.axis_size("c")
    z, x, c = lax.axis_index("z"), lax.axis_index("x"), lax.axis_index("c")
    dp_count = z_count * x_count * c_count
    dp_index = (z * x_count + x) * c_count + c
    band, width = old_factors.shape[2:]
    tile_count, row_count = gradients.shape[1:3]
    a_span = FF // width
    layer_blocks = a_span + D // width
    layers = tile_count // a_span
    old_flat = old_slots.reshape(dp_count)
    new_flat = new_slots.reshape(dp_count)
    own = lax.dynamic_index_in_dim(old_flat, dp_index, keepdims=False)
    own_block = jnp.maximum(own, 0)
    own_layer = own_block // layer_blocks
    own_input = own_block % layer_blocks < a_span

    rows = old_factors[0, 0]
    trace = jnp.trace(lax.dynamic_slice_in_dim(rows, mp_index * band, band, 1))
    bins = lax.broadcasted_iota(jnp.int32, (1, 128), 1)
    own_bin = jnp.where(own >= 0, 2 * own_layer + jnp.where(own_input, 0, 1), -1)
    binned = jnp.where(bins == own_bin, trace, 0.0)
    binned, rows = lax.optimization_barrier((binned, rows))
    binned = sum_of_all(binned, ("x", "c", "mp"), x_count * c_count * mp_count)
    binned, tiles = lax.optimization_barrier((binned, gradients[0]))
    binned = sum_of_all(binned, "z", z_count)
    trace_input = jnp.sum(jnp.where(bins == 2 * own_layer, binned, 0.0))
    trace_output = jnp.sum(jnp.where(bins == 2 * own_layer + 1, binned, 0.0))
    ratio = jnp.sqrt(trace_input / FF / (trace_output / D))
    shift = jnp.where(own_input, DAMPING_BASE * ratio, DAMPING_BASE / ratio)

    doubled = jnp.concatenate([rows, rows], axis=1)
    ahead = lax.dynamic_slice_in_dim(doubled, mp_index * band, 3 * band, 1)
    near = ahead[:, : 2 * band]
    far = jnp.concatenate([ahead[:, :band], ahead[:, 2 * band :]], axis=1)
    one = from_ahead(near, "mp", 1)
    two = from_ahead(near, "mp", 2)
    three = from_ahead(far, "mp", 3)

    block = jnp.maximum(old_flat, 0)
    tile_of = jnp.minimum(block // layer_blocks * a_span + block % layer_blocks, tile_count - 1)
    tile_of = tile_of.reshape(z_count, x_count, c_count).transpose(2, 1, 0)

    def tiles_of(core):
        index = lax.dynamic_index_in_dim(tile_of, core, keepdims=False)
        return take(tiles, index.reshape(-1))

    def split(value):
        return value.astype(jnp.float32).reshape(x_count, z_count, row_count, width)

    arrived = from_ahead(tiles_of(1 - c), "c", 1)
    partial = split(tiles_of(c)) + split(arrived)
    total = lax.dynamic_index_in_dim(partial, x, keepdims=False)
    for step in range(1, x_count):
        piece = lax.dynamic_index_in_dim(partial, (x + x_count - step) % x_count, keepdims=False)
        total = total + from_ahead(piece, "x", step)
    shift, total = lax.optimization_barrier((shift, total))
    tile = jnp.sum(exchange(total, "z"), axis=0).astype(jnp.bfloat16)

    scalars = jnp.stack([(own >= 0).astype(jnp.int32), mp_index.astype(jnp.int32)])
    inverse_band, inverse = invert(scalars, shift.reshape(1), rows, one, two, three)
    inverse_band, tile = lax.optimization_barrier((inverse_band, tile))

    def gather(value, axis, steps):
        return jnp.stack([value] + [from_ahead(value, axis, step) for step in steps])

    held = jnp.dot(tile, inverse, preferred_element_type=jnp.float32).astype(jnp.bfloat16)
    spread = exchange(inverse_band, DP)
    held = gather(gather(held, "z", (4, 8, 12)), "z", (1, 2, 15))
    slot_range = jnp.arange(dp_count, dtype=jnp.int32)
    empty = jnp.min(jnp.where(old_flat >= 0, dp_count - 1, slot_range))
    source = jnp.where(new_flat >= 0, positions(old_flat, new_flat), empty)
    outgoing, held = lax.optimization_barrier((pick(source, spread), held))
    arrived = exchange(outgoing, DP)
    arrived = arrived.reshape(band // ROWS, width // LANES, ROWS, LANES)
    inverses = arrived.transpose(0, 2, 1, 3).reshape(1, 1, band, width)
    held = gather(gather(held, "x", (1, 2, 3)), "c", (1,))
    held = held.reshape(dp_count, row_count, width)
    tile_range = jnp.arange(tile_count, dtype=jnp.int32)
    place = positions(old_flat, tile_range // a_span * layer_blocks + tile_range % a_span)
    far_z = (place // (x_count * c_count) - z + z_count) % z_count
    far_x = (place // c_count - x + x_count) % x_count
    far_c = (place - c + c_count) % c_count
    low = far_z % 4
    high = (far_z + jnp.where(low == 3, 1, 0)) // 4 % 4
    precond = take(held, ((far_c * x_count + far_x) * 4 + low) * 4 + high)
    return (inverses, precond)


def solution(mesh):
    dp_count, mp_count = mesh.devices.shape
    z_count = dp_count // (X_COUNT * CORES)
    parts = Mesh(
        mesh.devices.reshape(z_count, X_COUNT, CORES, mp_count), DP + ("mp",)
    )
    in_specs = (P(DP, None, "mp", None), P(DP, None, "mp", None), P(), P())
    out_specs = (P(DP, None, "mp", None), P(None, "mp", None))
    return jax.shard_map(local, mesh=parts, in_specs=in_specs, out_specs=out_specs, check_vma=False)
```

```python
import jax
import jax.numpy as jnp
from jax import lax
from jax.experimental import pallas as pl
from jax.experimental.pallas import tpu as pltpu
from jax.sharding import Mesh, PartitionSpec as P

D = 8192
FF = 28672
DAMPING_BASE = 2.0
X_COUNT, CORES = 4, 2
DP = ("z", "x", "c")

BASE = 32
SUB = 8
ROWS, LANES = 16, 128


def row_of(x, j):
    return jnp.broadcast_to(x[j : j + 1, :], x.shape)


def lane_of(x, j):
    return jnp.broadcast_to(x[:, j : j + 1], x.shape)


def reciprocal(x):
    return pltpu.reciprocal(x, approx=True)


def halves(x):
    high = x.astype(jnp.bfloat16)
    return high, (x - high.astype(jnp.float32)).astype(jnp.bfloat16)


def stacked(x, order, axis):
    parts = halves(x)
    return jnp.concatenate([parts[i] for i in order], axis=axis)


LEFT, RIGHT = (0, 0, 1), (0, 1, 0)


def dot(left, right):
    return jnp.dot(left, right, preferred_element_type=jnp.float32)


def invert_small(u, size):
    def at(i, j):
        return u[min(i, j), max(i, j)]

    for a in range(0, size, 2):
        b = a + 1
        aa, ab, bb = u[a, a], u[a, b], u[b, b]
        scale = reciprocal(aa * bb - ab * ab)
        others = [i for i in range(size) if i not in (a, b)]
        row_a = {i: bb * at(a, i) - ab * at(b, i) for i in others}
        row_b = {i: aa * at(b, i) - ab * at(a, i) for i in others}
        new = {(a, a): -bb * scale, (a, b): ab * scale, (b, b): -aa * scale}
        for i in others:
            new[min(a, i), max(a, i)] = row_a[i] * scale
            new[min(b, i), max(b, i)] = row_b[i] * scale
            for j in others:
                if i <= j:
                    cross = at(a, i) * row_a[j] + at(b, i) * row_b[j]
                    new[i, j] = u[i, j] - cross * scale
        u = new
    return u


def tree_sum(terms):
    while len(terms) > 1:
        terms = [a + b for a, b in zip(terms[::2], terms[1::2])]
    return terms[0]


def panel_sweep(groups, first):
    sub_ids = lax.broadcasted_iota(jnp.int32, (SUB, LANES), 0)
    lane_ids = lax.broadcasted_iota(jnp.int32, (SUB, LANES), 1)
    for p in range(len(groups)):
        tile, lane = divmod(first + p * SUB, LANES)
        pivot_lanes = (lane_ids // SUB) == lane // SUB
        spread = [lane_of(groups[p][tile], lane + j) for j in range(SUB)]
        u = {(i, j): row_of(spread[j], i) for j in range(SUB) for i in range(j + 1)}
        sources = []
        for j in range(SUB):
            line = [-row_of(x, j) for x in groups[p]]
            line[tile] = jnp.where(
                pivot_lanes, jnp.where(lane_ids == lane + j, 1.0, 0.0), line[tile]
            )
            sources.append(line)
        u = invert_small(u, SUB)
        tiles = range(len(groups[p]))
        lines = [
            [
                tree_sum([u[min(i, j), max(i, j)] * sources[j][t] for j in range(SUB)])
                for t in tiles
            ]
            for i in range(SUB)
        ]
        for g in range(len(groups)):
            if g == p:
                continue
            factors = [lane_of(groups[g][tile], lane + j) for j in range(SUB)]
            for t in tiles:
                kept = groups[g][t]
                if t == tile:
                    kept = jnp.where(pivot_lanes, 0.0, kept)
                groups[g][t] = kept - tree_sum([factors[j] * lines[j][t] for j in range(SUB)])
        for t in tiles:
            row = lines[0][t]
            for j in range(1, SUB):
                row = jnp.where(sub_ids == j, lines[j][t], row)
            groups[p][t] = row
    return groups


def block_sweep(d_ref):
    wide = d_ref.shape[0]
    lane_ids = lax.broadcasted_iota(jnp.int32, (wide, wide), 1)
    for first in range(0, wide, BASE):
        old = d_ref[first : first + BASE, :]
        groups = [
            [old[g : g + SUB, t : t + LANES] for t in range(0, wide, LANES)]
            for g in range(0, BASE, SUB)
        ]
        groups = panel_sweep(groups, first)
        new = jnp.concatenate([jnp.concatenate(g, axis=1) for g in groups], axis=0)
        update = lax.dot_general(
            stacked(old, LEFT, 0),
            stacked(new, RIGHT, 0),
            (((0,), (0,)), ((), ())),
            preferred_element_type=jnp.float32,
        )
        kept = jnp.where(lane_ids // BASE == first // BASE, 0.0, d_ref[...])
        d_ref[...] = kept - update
        d_ref[first : first + BASE, :] = new


def invert_kernel(
    scalar_ref, traces_ref, rows_hbm, one_hbm, two_hbm, three_hbm,
    band_hbm, full_ref, m_ref, d_ref, left_ref, right_ref, band_ref, in_sems, out_sem,
):
    wide, n = rows_hbm.shape
    count = n // wide
    mp_index = scalar_ref[1]

    def block(i):
        return slice(i * wide, (i + 1) * wide)

    def place(i):
        return pl.ds(pl.multiple_of(lax.rem(mp_index + i, count) * wide, wide), wide)

    @pl.when(scalar_ref[0] > 0)
    def _():
        arrivals = [(rows_hbm.at[:, place(j)], 0, j) for j in range(count)]
        for i, source in enumerate((one_hbm, two_hbm, three_hbm)):
            arrivals.append((source.at[:, block(0)], i + 1, i + 1))
            arrivals.append((source.at[:, block(1)], i + 1, (i + 1) % (count - 1) + 1))
        copies = [
            pltpu.make_async_copy(source, m_ref.at[block(i), block(j)], in_sems.at[at])
            for at, (source, i, j) in enumerate(arrivals)
        ]
        for copy in copies:
            copy.start()

        traces = jnp.sum(traces_ref[...], axis=0, keepdims=True)
        lane_ids = lax.broadcasted_iota(jnp.int32, traces.shape, 1)

        def pick_lane(lane):
            return jnp.sum(jnp.where(lane_ids == lane, traces, 0.0), axis=1, keepdims=True)

        lane = 2 * scalar_ref[2]
        ratio = jnp.sqrt(pick_lane(lane) / FF / (pick_lane(lane + 1) / D))
        shift = jnp.where(scalar_ref[3] > 0, DAMPING_BASE * ratio, DAMPING_BASE / ratio)
        diagonal = lax.broadcasted_iota(jnp.int32, (wide, wide), 0) == lax.broadcasted_iota(
            jnp.int32, (wide, wide), 1
        )
        for copy in copies:
            copy.wait()

        total = jnp.zeros((wide, wide), jnp.float32)
        for i in range(count):
            total = total + jnp.where(diagonal, m_ref[block(i), block(i)] + shift, 0.0)
        total = jnp.sum(jnp.sum(total, axis=0, keepdims=True), axis=1, keepdims=True)
        scale = n / total
        for _, i, j in arrivals:
            value = m_ref[block(i), block(j)]
            if i == j:
                m_ref[block(i), block(i)] = jnp.where(diagonal, value + shift, value) * scale
            else:
                value = value * scale
                m_ref[block(i), block(j)] = value
                m_ref[block(j), block(i)] = value.T

        @pl.loop(0, count)
        def _(k):
            at = pl.ds(pl.multiple_of(k * wide, wide), wide)
            d_ref[...] = m_ref[at, at]
            block_sweep(d_ref)

            left_ref[...] = stacked(m_ref[:, at], LEFT, 1)
            right_ref[...] = stacked(m_ref[at, :], RIGHT, 0)
            rows = -dot(stacked(d_ref[...], LEFT, 1), right_ref[...])
            m_ref[:, at] = jnp.zeros((n, wide), jnp.float32)
            m_ref[at, :] = rows
            m_ref[at, at] = d_ref[...]
            right_ref[...] = stacked(m_ref[at, :], RIGHT, 0)
            for i in range(count):

                @pl.when(i != k)
                def _():
                    m_ref[block(i), :] = m_ref[block(i), :] - dot(left_ref[block(i), :], right_ref[...])

        for j in range(count):
            band = (m_ref[block(0), block(j)] * -scale).astype(jnp.bfloat16)
            for r in range(wide // ROWS):
                for c in range(wide // LANES):
                    at = lax.rem(mp_index + j, count) * (wide // LANES) + r * (n // LANES) + c
                    band_ref[at] = band[r * ROWS : (r + 1) * ROWS, c * LANES : (c + 1) * LANES]
        sent = pltpu.make_async_copy(band_ref, band_hbm, out_sem)
        sent.start()
        for j in range(count):
            for i in range(count):
                full_ref[place(i), place(j)] = (m_ref[block(i), block(j)] * -scale).astype(jnp.bfloat16)
        sent.wait()

    @pl.when(scalar_ref[0] <= 0)
    def _():
        band_ref[...] = jnp.zeros(band_ref.shape, jnp.bfloat16)
        full_ref[...] = jnp.zeros(full_ref.shape, jnp.bfloat16)
        sent = pltpu.make_async_copy(band_ref, band_hbm, out_sem)
        sent.start()
        sent.wait()


def invert(scalars, traces, rows, one, two, three):
    wide, n = rows.shape
    in_smem = pl.BlockSpec(memory_space=pltpu.SMEM)
    in_vmem = pl.BlockSpec(memory_space=pltpu.VMEM)
    in_hbm = pl.BlockSpec(memory_space=pltpu.HBM)
    pieces = (wide * n // (ROWS * LANES), ROWS, LANES)
    return pl.pallas_call(
        invert_kernel,
        out_shape=(
            jax.ShapeDtypeStruct(pieces, jnp.bfloat16),
            jax.ShapeDtypeStruct((n, n), jnp.bfloat16),
        ),
        in_specs=[in_smem, in_vmem] + [in_hbm] * 4,
        out_specs=(in_hbm, in_vmem),
        scratch_shapes=[
            pltpu.VMEM((n, n), jnp.float32),
            pltpu.VMEM((wide, wide), jnp.float32),
            pltpu.VMEM((n, 3 * wide), jnp.bfloat16),
            pltpu.VMEM((3 * wide, n), jnp.bfloat16),
            pltpu.VMEM(pieces, jnp.bfloat16),
            pltpu.SemaphoreType.DMA((10,)),
            pltpu.SemaphoreType.DMA,
        ],
        compiler_params=pltpu.CompilerParams(vmem_limit_bytes=24 * 1024 * 1024),
        cost_estimate=pl.CostEstimate(
            flops=36 * n * n * n, bytes_accessed=6 * n * n, transcendentals=0
        ),
    )(scalars, traces, rows, one, two, three)


def prepare_kernel(mp_ref, rows_ref, near_ref, far_ref, trace_ref):
    wide, n = rows_ref.shape

    def place(i):
        return pl.ds(pl.multiple_of(lax.rem(mp_ref[0] + i, n // wide) * wide, wide), wide)

    own = rows_ref[:, place(0)]
    diagonal = lax.broadcasted_iota(jnp.int32, own.shape, 0) == lax.broadcasted_iota(
        jnp.int32, own.shape, 1
    )
    trace = jnp.sum(jnp.where(diagonal, own, 0.0), axis=0, keepdims=True)
    trace = jnp.sum(trace, axis=1, keepdims=True)
    trace_ref[...] = jnp.broadcast_to(trace[None], trace_ref.shape)
    near_ref[:, :wide] = own
    near_ref[:, wide:] = rows_ref[:, place(1)]
    far_ref[:, :wide] = own
    far_ref[:, wide:] = rows_ref[:, place(2)]


def prepare(mp_index, rows, copies):
    wide, n = rows.shape
    in_vmem = pl.BlockSpec(memory_space=pltpu.VMEM)
    return pl.pallas_call(
        prepare_kernel,
        out_shape=(
            jax.ShapeDtypeStruct((wide, 2 * wide), jnp.float32),
            jax.ShapeDtypeStruct((wide, 2 * wide), jnp.float32),
            jax.ShapeDtypeStruct((copies, 1, LANES), jnp.float32),
        ),
        in_specs=[pl.BlockSpec(memory_space=pltpu.SMEM), in_vmem],
        out_specs=(in_vmem,) * 3,
        compiler_params=pltpu.CompilerParams(vmem_limit_bytes=8 * 1024 * 1024),
    )(mp_index.reshape(1).astype(jnp.int32), rows)


def pick_kernel(index_ref, src_ref, out_ref):
    @pl.loop(0, out_ref.shape[0], unroll=8)
    def _(i):
        out_ref[i] = src_ref[index_ref[i]]


def pick(index, source):
    in_vmem = pl.BlockSpec(memory_space=pltpu.VMEM)
    return pl.pallas_call(
        pick_kernel,
        out_shape=jax.ShapeDtypeStruct(index.shape + source.shape[1:], source.dtype),
        in_specs=[pl.BlockSpec(memory_space=pltpu.SMEM), in_vmem],
        out_specs=in_vmem,
        compiler_params=pltpu.CompilerParams(vmem_limit_bytes=4 * 1024 * 1024),
    )(index, source)


def take(source, index):
    return source.at[index].get(mode="promise_in_bounds")


def positions(slot_ids, wanted):
    slot_range = jnp.arange(slot_ids.shape[0], dtype=jnp.int32)
    hit = slot_ids[None, :] == wanted[:, None]
    return jnp.sum(jnp.where(hit, slot_range[None, :], 0), axis=1).astype(jnp.int32)


def exchange(pieces, axes):
    return lax.all_to_all(pieces, axes, split_axis=0, concat_axis=0, tiled=True)


def from_ahead(value, axis, step):
    count = lax.axis_size(axis)
    return lax.ppermute(value, axis, [((i + step) % count, i) for i in range(count)])


def local(old_factors, gradients, old_slots, new_slots):
    mp_index = lax.axis_index("mp")
    mp_count = lax.axis_size("mp")
    z_count, x_count, c_count = lax.axis_size("z"), lax.axis_size("x"), lax.axis_size("c")
    z, x, c = lax.axis_index("z"), lax.axis_index("x"), lax.axis_index("c")
    dp_count = z_count * x_count * c_count
    dp_index = (z * x_count + x) * c_count + c
    band, width = old_factors.shape[2:]
    tile_count, row_count = gradients.shape[1:3]
    a_span = FF // width
    layer_blocks = a_span + D // width
    layers = tile_count // a_span
    old_flat = old_slots.reshape(dp_count)
    new_flat = new_slots.reshape(dp_count)
    own = lax.dynamic_index_in_dim(old_flat, dp_index, keepdims=False)
    own_block = jnp.maximum(own, 0)
    own_layer = own_block // layer_blocks
    own_input = own_block % layer_blocks < a_span

    rows = old_factors[0, 0]
    near, far, trace = prepare(mp_index, rows, x_count * c_count * mp_count)
    trace = exchange(trace, ("x", "c", "mp")).reshape(x_count * c_count, mp_count, LANES)
    plane = lax.dynamic_slice_in_dim(old_flat, z * x_count * c_count, x_count * c_count)
    plane_bin = 2 * (plane // layer_blocks) + jnp.where(plane % layer_blocks < a_span, 0, 1)
    plane_bin = jnp.where(plane >= 0, plane_bin, -1)
    lane_ids = lax.broadcasted_iota(jnp.int32, (1, 1, LANES), 2)
    binned = jnp.sum(jnp.where(lane_ids == plane_bin[:, None, None], trace, 0.0), axis=(0, 1))
    binned, near, far, tiles = lax.optimization_barrier((binned, near, far, gradients[0]))
    binned = jnp.broadcast_to(binned[None, None], (z_count, 1, LANES))
    traces = exchange(binned, "z").reshape(z_count, LANES)

    one = from_ahead(near, "mp", 1)
    two = from_ahead(near, "mp", 2)
    three = from_ahead(far, "mp", 3)

    block = jnp.maximum(old_flat, 0)
    tile_of = jnp.minimum(block // layer_blocks * a_span + block % layer_blocks, tile_count - 1)
    tile_of = tile_of.reshape(z_count * x_count, c_count)

    def tiles_of(core):
        return take(tiles, lax.dynamic_index_in_dim(tile_of, core, 1, keepdims=False))

    arrived = from_ahead(tiles_of(1 - c), "c", 1)
    partial = tiles_of(c).astype(jnp.float32) + arrived.astype(jnp.float32)
    partial, traces = lax.optimization_barrier((partial.astype(jnp.bfloat16), traces))
    partial = exchange(partial, ("z", "x"))
    tile = jnp.sum(partial.astype(jnp.float32), axis=0).astype(jnp.bfloat16)

    scalars = jnp.stack(
        [v.astype(jnp.int32) for v in (own >= 0, mp_index, own_layer, own_input)]
    )
    inverse_band, inverse = invert(scalars, traces, rows, one, two, three)
    inverse_band, tile = lax.optimization_barrier((inverse_band, tile))

    def gather(value, axis, steps):
        return jnp.stack([value] + [from_ahead(value, axis, step) for step in steps])

    held = jnp.dot(tile, inverse, preferred_element_type=jnp.float32).astype(jnp.bfloat16)
    held = gather(held, "z", (4, 8, 12))
    inverse_band, held = lax.optimization_barrier((inverse_band, held))
    spread = exchange(inverse_band, DP)
    held = gather(held, "z", (1, 2, 15))
    slot_range = jnp.arange(dp_count, dtype=jnp.int32)
    empty = jnp.min(jnp.where(old_flat >= 0, dp_count - 1, slot_range))
    source = jnp.where(new_flat >= 0, positions(old_flat, new_flat), empty)
    outgoing, held = lax.optimization_barrier((pick(source, spread), held))
    arrived = exchange(outgoing, DP)
    arrived = arrived.reshape(band // ROWS, width // LANES, ROWS, LANES)
    inverses = arrived.transpose(0, 2, 1, 3).reshape(1, 1, band, width)
    held = gather(gather(held, "x", (1, 2, 3)), "c", (1,))
    held = held.reshape(dp_count, row_count, width)
    tile_range = jnp.arange(tile_count, dtype=jnp.int32)
    place = positions(old_flat, tile_range // a_span * layer_blocks + tile_range % a_span)
    far_z = (place // (x_count * c_count) - z + z_count) % z_count
    far_x = (place // c_count - x + x_count) % x_count
    far_c = (place - c + c_count) % c_count
    low = far_z % 4
    high = (far_z + jnp.where(low == 3, 1, 0)) // 4 % 4
    precond = take(held, ((far_c * x_count + far_x) * 4 + low) * 4 + high)
    return (inverses, precond)


def solution(mesh):
    dp_count, mp_count = mesh.devices.shape
    z_count = dp_count // (X_COUNT * CORES)
    parts = Mesh(
        mesh.devices.reshape(z_count, X_COUNT, CORES, mp_count), DP + ("mp",)
    )
    in_specs = (P(DP, None, "mp", None), P(DP, None, "mp", None), P(), P())
    out_specs = (P(DP, None, "mp", None), P(None, "mp", None))
    return jax.shard_map(local, mesh=parts, in_specs=in_specs, out_specs=out_specs, check_vma=False)
```

```python
import jax
import jax.numpy as jnp
from jax import lax
from jax.experimental import pallas as pl
from jax.experimental.pallas import tpu as pltpu
from jax.sharding import Mesh, PartitionSpec as P

D = 8192
FF = 28672
DAMPING_BASE = 2.0
X_COUNT, CORES = 4, 2
DP = ("z", "x", "c")

BASE = 32
SUB = 8
ROWS, LANES = 16, 128


def row_of(x, j):
    return jnp.broadcast_to(x[j : j + 1, :], x.shape)


def lane_of(x, j):
    return jnp.broadcast_to(x[:, j : j + 1], x.shape)


def reciprocal(x):
    return pltpu.reciprocal(x, approx=True)


def halves(x):
    high = x.astype(jnp.bfloat16)
    return high, (x - high.astype(jnp.float32)).astype(jnp.bfloat16)


def stacked(x, order, axis):
    parts = halves(x)
    return jnp.concatenate([parts[i] for i in order], axis=axis)


LEFT, RIGHT = (0, 0, 1), (0, 1, 0)


def dot(left, right):
    return jnp.dot(left, right, preferred_element_type=jnp.float32)


def invert_small(u, size):
    def at(i, j):
        return u[min(i, j), max(i, j)]

    for a in range(0, size, 2):
        b = a + 1
        aa, ab, bb = u[a, a], u[a, b], u[b, b]
        scale = reciprocal(aa * bb - ab * ab)
        others = [i for i in range(size) if i not in (a, b)]
        row_a = {i: bb * at(a, i) - ab * at(b, i) for i in others}
        row_b = {i: aa * at(b, i) - ab * at(a, i) for i in others}
        new = {(a, a): -bb * scale, (a, b): ab * scale, (b, b): -aa * scale}
        for i in others:
            new[min(a, i), max(a, i)] = row_a[i] * scale
            new[min(b, i), max(b, i)] = row_b[i] * scale
            for j in others:
                if i <= j:
                    cross = at(a, i) * row_a[j] + at(b, i) * row_b[j]
                    new[i, j] = u[i, j] - cross * scale
        u = new
    return u


def tree_sum(terms):
    while len(terms) > 1:
        terms = [a + b for a, b in zip(terms[::2], terms[1::2])]
    return terms[0]


def panel_sweep(groups, starts):
    sub_ids = lax.broadcasted_iota(jnp.int32, (SUB, LANES), 0)
    lane_ids = lax.broadcasted_iota(jnp.int32, (SUB, LANES), 1)
    tiles = range(len(starts))
    from_start = [lane_ids - start for start in starts]
    for p in range(len(groups)):
        lane = p * SUB
        places = [x - lane for x in from_start]
        pivot_lanes = [(x >= 0) & (x < SUB) for x in places]
        spread = [lane_of(groups[p][-1], lane + j) for j in range(SUB)]
        u = {(i, j): row_of(spread[j], i) for j in range(SUB) for i in range(j + 1)}
        sources = [
            [
                jnp.where(
                    pivot_lanes[t], jnp.where(places[t] == j, 1.0, 0.0), -row_of(groups[p][t], j)
                )
                for t in tiles
            ]
            for j in range(SUB)
        ]
        u = invert_small(u, SUB)
        lines = [
            [
                tree_sum([u[min(i, j), max(i, j)] * sources[j][t] for j in range(SUB)])
                for t in tiles
            ]
            for i in range(SUB)
        ]
        for g in range(len(groups)):
            if g == p:
                continue
            factors = [lane_of(groups[g][-1], lane + j) for j in range(SUB)]
            for t in tiles:
                kept = jnp.where(pivot_lanes[t], 0.0, groups[g][t])
                groups[g][t] = kept - tree_sum([factors[j] * lines[j][t] for j in range(SUB)])
        for t in tiles:
            row = lines[0][t]
            for j in range(1, SUB):
                row = jnp.where(sub_ids == j, lines[j][t], row)
            groups[p][t] = row
    return groups


def block_sweep(d_ref):
    wide = d_ref.shape[0]
    lane_ids = lax.broadcasted_iota(jnp.int32, (wide, wide), 1)

    @pl.loop(0, wide // BASE)
    def _(q):
        first = q * BASE
        rows = pl.ds(pl.multiple_of(first, BASE), BASE)
        old = d_ref[rows, :]
        tile = pl.ds(pl.multiple_of(first // LANES * LANES, LANES), LANES)
        start = lax.rem(first, LANES)
        own = pltpu.roll(d_ref[rows, tile], lax.rem(LANES - start, LANES), 1)
        groups = [
            [old[g : g + SUB, t : t + LANES] for t in range(0, wide, LANES)] + [own[g : g + SUB]]
            for g in range(0, BASE, SUB)
        ]
        groups = panel_sweep(groups, [first - t for t in range(0, wide, LANES)] + [0])
        new = jnp.concatenate([jnp.concatenate(g[:-1], axis=1) for g in groups], axis=0)
        update = lax.dot_general(
            stacked(old, LEFT, 0),
            stacked(new, RIGHT, 0),
            (((0,), (0,)), ((), ())),
            preferred_element_type=jnp.float32,
        )
        d_ref[...] = jnp.where(lane_ids // BASE == q, 0.0, d_ref[...]) - update
        d_ref[rows, :] = new


def invert_kernel(
    scalar_ref, traces_ref, rows_hbm, one_hbm, two_hbm, three_hbm,
    band_hbm, full_ref, m_ref, d_ref, left_ref, right_ref, band_ref, in_sems, out_sem,
):
    wide, n = rows_hbm.shape
    count = n // wide
    mp_index = scalar_ref[1]

    def block(i):
        return slice(i * wide, (i + 1) * wide)

    def place(i):
        return pl.ds(pl.multiple_of(lax.rem(mp_index + i, count) * wide, wide), wide)

    @pl.when(scalar_ref[0] > 0)
    def _():
        arrivals = [(rows_hbm.at[:, place(j)], 0, j) for j in range(count)]
        for i, source in enumerate((one_hbm, two_hbm, three_hbm)):
            arrivals.append((source.at[:, block(0)], i + 1, i + 1))
            arrivals.append((source.at[:, block(1)], i + 1, (i + 1) % (count - 1) + 1))
        copies = [
            pltpu.make_async_copy(source, m_ref.at[block(i), block(j)], in_sems.at[at])
            for at, (source, i, j) in enumerate(arrivals)
        ]
        for copy in copies:
            copy.start()

        traces = jnp.sum(traces_ref[...], axis=0, keepdims=True)
        lane_ids = lax.broadcasted_iota(jnp.int32, traces.shape, 1)

        def pick_lane(lane):
            return jnp.sum(jnp.where(lane_ids == lane, traces, 0.0), axis=1, keepdims=True)

        lane = 2 * scalar_ref[2]
        ratio = jnp.sqrt(pick_lane(lane) / FF / (pick_lane(lane + 1) / D))
        shift = jnp.where(scalar_ref[3] > 0, DAMPING_BASE * ratio, DAMPING_BASE / ratio)
        diagonal = lax.broadcasted_iota(jnp.int32, (wide, wide), 0) == lax.broadcasted_iota(
            jnp.int32, (wide, wide), 1
        )
        for copy in copies:
            copy.wait()

        total = jnp.zeros((wide, wide), jnp.float32)
        for i in range(count):
            total = total + jnp.where(diagonal, m_ref[block(i), block(i)] + shift, 0.0)
        total = jnp.sum(jnp.sum(total, axis=0, keepdims=True), axis=1, keepdims=True)
        scale = n / total
        def part(i):
            return pl.ds(pl.multiple_of(i * wide, wide), wide)

        def settle(i, j):
            value = m_ref[part(i), part(j)] * scale
            m_ref[part(i), part(j)] = value
            m_ref[part(j), part(i)] = value.T

        @pl.loop(0, count)
        def _(i):
            value = m_ref[part(i), part(i)]
            m_ref[part(i), part(i)] = jnp.where(diagonal, value + shift, value) * scale

        @pl.loop(1, count)
        def _(i):
            settle(0, i)

        @pl.loop(1, count)
        def _(i):
            settle(i, lax.rem(i, count - 1) + 1)

        @pl.loop(0, count)
        def _(k):
            at = part(k)
            d_ref[...] = m_ref[at, at]
            block_sweep(d_ref)

            @pl.loop(0, count)
            def _(i):
                left_ref[part(i), :] = stacked(m_ref[part(i), at], LEFT, 1)
                right_ref[:, part(i)] = stacked(m_ref[at, part(i)], RIGHT, 0)

            pivot_left = stacked(d_ref[...], LEFT, 1)

            @pl.loop(0, count)
            def _(j):
                m_ref[at, part(j)] = -dot(pivot_left, right_ref[:, part(j)])

            @pl.loop(0, count)
            def _(i):
                m_ref[part(i), at] = jnp.zeros((wide, wide), jnp.float32)

            m_ref[at, at] = d_ref[...]

            @pl.loop(0, count)
            def _(j):
                right_ref[:, part(j)] = stacked(m_ref[at, part(j)], RIGHT, 0)

            @pl.loop(1, count)
            def _(step):
                i = part(lax.rem(k + step, count))

                @pl.loop(0, count // 2)
                def _(j):
                    half = pl.ds(pl.multiple_of(j * 2 * wide, 2 * wide), 2 * wide)
                    m_ref[i, half] = m_ref[i, half] - dot(left_ref[i, :], right_ref[:, half])

        @pl.loop(0, count)
        def _(j):
            band = (m_ref[block(0), part(j)] * -scale).astype(jnp.bfloat16)
            first = lax.rem(mp_index + j, count) * (wide // LANES)
            for r in range(wide // ROWS):
                for c in range(wide // LANES):
                    band_ref[first + r * (n // LANES) + c] = band[
                        r * ROWS : (r + 1) * ROWS, c * LANES : (c + 1) * LANES
                    ]

        sent = pltpu.make_async_copy(band_ref, band_hbm, out_sem)
        sent.start()

        @pl.loop(0, count)
        def _(i):
            @pl.loop(0, count)
            def _(j):
                full_ref[place(i), place(j)] = (m_ref[part(i), part(j)] * -scale).astype(jnp.bfloat16)

        sent.wait()

    @pl.when(scalar_ref[0] <= 0)
    def _():
        band_ref[...] = jnp.zeros(band_ref.shape, jnp.bfloat16)
        full_ref[...] = jnp.zeros(full_ref.shape, jnp.bfloat16)
        sent = pltpu.make_async_copy(band_ref, band_hbm, out_sem)
        sent.start()
        sent.wait()


def invert(scalars, traces, rows, one, two, three):
    wide, n = rows.shape
    in_smem = pl.BlockSpec(memory_space=pltpu.SMEM)
    in_vmem = pl.BlockSpec(memory_space=pltpu.VMEM)
    in_hbm = pl.BlockSpec(memory_space=pltpu.HBM)
    pieces = (wide * n // (ROWS * LANES), ROWS, LANES)
    return pl.pallas_call(
        invert_kernel,
        out_shape=(
            jax.ShapeDtypeStruct(pieces, jnp.bfloat16),
            jax.ShapeDtypeStruct((n, n), jnp.bfloat16),
        ),
        in_specs=[in_smem, in_vmem] + [in_hbm] * 4,
        out_specs=(in_hbm, in_vmem),
        scratch_shapes=[
            pltpu.VMEM((n, n), jnp.float32),
            pltpu.VMEM((wide, wide), jnp.float32),
            pltpu.VMEM((n, 3 * wide), jnp.bfloat16),
            pltpu.VMEM((3 * wide, n), jnp.bfloat16),
            pltpu.VMEM(pieces, jnp.bfloat16),
            pltpu.SemaphoreType.DMA((10,)),
            pltpu.SemaphoreType.DMA,
        ],
        compiler_params=pltpu.CompilerParams(vmem_limit_bytes=56 * 1024 * 1024),
        cost_estimate=pl.CostEstimate(
            flops=36 * n * n * n, bytes_accessed=6 * n * n, transcendentals=0
        ),
    )(scalars, traces, rows, one, two, three)


def prepare_kernel(mp_ref, rows_ref, near_ref, far_ref, trace_ref):
    wide, n = rows_ref.shape

    def place(i):
        return pl.ds(pl.multiple_of(lax.rem(mp_ref[0] + i, n // wide) * wide, wide), wide)

    own = rows_ref[:, place(0)]
    diagonal = lax.broadcasted_iota(jnp.int32, own.shape, 0) == lax.broadcasted_iota(
        jnp.int32, own.shape, 1
    )
    trace = jnp.sum(jnp.where(diagonal, own, 0.0), axis=0, keepdims=True)
    trace = jnp.sum(trace, axis=1, keepdims=True)
    trace_ref[...] = jnp.broadcast_to(trace[None], trace_ref.shape)
    near_ref[:, :wide] = own
    near_ref[:, wide:] = rows_ref[:, place(1)]
    far_ref[:, :wide] = own
    far_ref[:, wide:] = rows_ref[:, place(2)]


def prepare(mp_index, rows, copies):
    wide, n = rows.shape
    in_vmem = pl.BlockSpec(memory_space=pltpu.VMEM)
    return pl.pallas_call(
        prepare_kernel,
        out_shape=(
            jax.ShapeDtypeStruct((wide, 2 * wide), jnp.float32),
            jax.ShapeDtypeStruct((wide, 2 * wide), jnp.float32),
            jax.ShapeDtypeStruct((copies, 1, LANES), jnp.float32),
        ),
        in_specs=[pl.BlockSpec(memory_space=pltpu.SMEM), in_vmem],
        out_specs=(in_vmem,) * 3,
        compiler_params=pltpu.CompilerParams(vmem_limit_bytes=8 * 1024 * 1024),
    )(mp_index.reshape(1).astype(jnp.int32), rows)


def pick_kernel(index_ref, src_ref, out_ref):
    @pl.loop(0, out_ref.shape[0], unroll=8)
    def _(i):
        out_ref[i] = src_ref[index_ref[i]]


def pick(index, source):
    in_vmem = pl.BlockSpec(memory_space=pltpu.VMEM)
    return pl.pallas_call(
        pick_kernel,
        out_shape=jax.ShapeDtypeStruct(index.shape + source.shape[1:], source.dtype),
        in_specs=[pl.BlockSpec(memory_space=pltpu.SMEM), in_vmem],
        out_specs=in_vmem,
        compiler_params=pltpu.CompilerParams(vmem_limit_bytes=4 * 1024 * 1024),
    )(index, source)


def take(source, index):
    return source.at[index].get(mode="promise_in_bounds")


def positions(slot_ids, wanted):
    slot_range = jnp.arange(slot_ids.shape[0], dtype=jnp.int32)
    hit = slot_ids[None, :] == wanted[:, None]
    return jnp.sum(jnp.where(hit, slot_range[None, :], 0), axis=1).astype(jnp.int32)


def exchange(pieces, axes):
    return lax.all_to_all(pieces, axes, split_axis=0, concat_axis=0, tiled=True)


def from_ahead(value, axis, step):
    count = lax.axis_size(axis)
    return lax.ppermute(value, axis, [((i + step) % count, i) for i in range(count)])


def local(old_factors, gradients, old_slots, new_slots):
    mp_index = lax.axis_index("mp")
    mp_count = lax.axis_size("mp")
    z_count, x_count, c_count = lax.axis_size("z"), lax.axis_size("x"), lax.axis_size("c")
    z, x, c = lax.axis_index("z"), lax.axis_index("x"), lax.axis_index("c")
    dp_count = z_count * x_count * c_count
    dp_index = (z * x_count + x) * c_count + c
    band, width = old_factors.shape[2:]
    tile_count, row_count = gradients.shape[1:3]
    a_span = FF // width
    layer_blocks = a_span + D // width
    layers = tile_count // a_span
    old_flat = old_slots.reshape(dp_count)
    new_flat = new_slots.reshape(dp_count)
    own = lax.dynamic_index_in_dim(old_flat, dp_index, keepdims=False)
    own_block = jnp.maximum(own, 0)
    own_layer = own_block // layer_blocks
    own_input = own_block % layer_blocks < a_span

    rows = old_factors[0, 0]
    near, far, trace = prepare(mp_index, rows, x_count * c_count * mp_count)
    trace = exchange(trace, ("x", "c", "mp")).reshape(x_count * c_count, mp_count, LANES)
    plane = lax.dynamic_slice_in_dim(old_flat, z * x_count * c_count, x_count * c_count)
    plane_bin = 2 * (plane // layer_blocks) + jnp.where(plane % layer_blocks < a_span, 0, 1)
    plane_bin = jnp.where(plane >= 0, plane_bin, -1)
    lane_ids = lax.broadcasted_iota(jnp.int32, (1, 1, LANES), 2)
    binned = jnp.sum(jnp.where(lane_ids == plane_bin[:, None, None], trace, 0.0), axis=(0, 1))
    binned, near, far, tiles = lax.optimization_barrier((binned, near, far, gradients[0]))
    binned = jnp.broadcast_to(binned[None, None], (z_count, 1, LANES))
    traces = exchange(binned, "z").reshape(z_count, LANES)

    one = from_ahead(near, "mp", 1)
    two = from_ahead(near, "mp", 2)
    three = from_ahead(far, "mp", 3)

    block = jnp.maximum(old_flat, 0)
    tile_of = jnp.minimum(block // layer_blocks * a_span + block % layer_blocks, tile_count - 1)
    tile_of = tile_of.reshape(z_count * x_count, c_count)

    def tiles_of(core):
        return take(tiles, lax.dynamic_index_in_dim(tile_of, core, 1, keepdims=False))

    arrived = from_ahead(tiles_of(1 - c), "c", 1)
    partial = tiles_of(c).astype(jnp.float32) + arrived.astype(jnp.float32)
    partial, traces = lax.optimization_barrier((partial.astype(jnp.bfloat16), traces))
    partial = exchange(partial, ("z", "x"))
    tile = jnp.sum(partial.astype(jnp.float32), axis=0).astype(jnp.bfloat16)

    scalars = jnp.stack(
        [v.astype(jnp.int32) for v in (own >= 0, mp_index, own_layer, own_input)]
    )
    inverse_band, inverse = invert(scalars, traces, rows, one, two, three)
    inverse_band, tile = lax.optimization_barrier((inverse_band, tile))

    def gather(value, axis, steps):
        return jnp.stack([value] + [from_ahead(value, axis, step) for step in steps])

    held = jnp.dot(tile, inverse, preferred_element_type=jnp.float32).astype(jnp.bfloat16)
    held = exchange(jnp.broadcast_to(held[None], (z_count,) + held.shape), "z")
    inverse_band, held = lax.optimization_barrier((inverse_band, held))
    spread = exchange(inverse_band, DP)
    held = gather(gather(held, "x", (1, 2, 3)), "c", (1,))
    slot_range = jnp.arange(dp_count, dtype=jnp.int32)
    empty = jnp.min(jnp.where(old_flat >= 0, dp_count - 1, slot_range))
    source = jnp.where(new_flat >= 0, positions(old_flat, new_flat), empty)
    outgoing, held = lax.optimization_barrier((pick(source, spread), held))
    arrived = exchange(outgoing, DP)
    arrived = arrived.reshape(band // ROWS, width // LANES, ROWS, LANES)
    inverses = arrived.transpose(0, 2, 1, 3).reshape(1, 1, band, width)
    held = held.reshape(dp_count, row_count, width)
    tile_range = jnp.arange(tile_count, dtype=jnp.int32)
    place = positions(old_flat, tile_range // a_span * layer_blocks + tile_range % a_span)
    far_x = (place // c_count - x + x_count) % x_count
    far_c = (place - c + c_count) % c_count
    from_z = place // (x_count * c_count)
    precond = take(held, (far_c * x_count + far_x) * z_count + from_z)
    return (inverses, precond)


def solution(mesh):
    dp_count, mp_count = mesh.devices.shape
    z_count = dp_count // (X_COUNT * CORES)
    parts = Mesh(
        mesh.devices.reshape(z_count, X_COUNT, CORES, mp_count), DP + ("mp",)
    )
    in_specs = (P(DP, None, "mp", None), P(DP, None, "mp", None), P(), P())
    out_specs = (P(DP, None, "mp", None), P(None, "mp", None))
    return jax.shard_map(local, mesh=parts, in_specs=in_specs, out_specs=out_specs, check_vma=False)
```

```python
import jax
import jax.numpy as jnp
from jax import lax
from jax.experimental import pallas as pl
from jax.experimental.pallas import tpu as pltpu
from jax.sharding import Mesh, PartitionSpec as P

D = 8192
FF = 28672
DAMPING_BASE = 2.0
X_COUNT, CORES = 4, 2
DP = ("z", "x", "c")

BASE = 32
SUB = 8
ROWS, LANES = 16, 128


def row_of(x, j):
    return jnp.broadcast_to(x[j : j + 1, :], x.shape)


def lane_of(x, j):
    return jnp.broadcast_to(x[:, j : j + 1], x.shape)


def reciprocal(x):
    return pltpu.reciprocal(x, approx=True)


def halves(x):
    high = x.astype(jnp.bfloat16)
    return high, (x - high.astype(jnp.float32)).astype(jnp.bfloat16)


def stacked(x, order, axis):
    parts = halves(x)
    return jnp.concatenate([parts[i] for i in order], axis=axis)


LEFT, RIGHT = (0, 0, 1), (0, 1, 0)


def dot(left, right):
    return jnp.dot(left, right, preferred_element_type=jnp.float32)


def solve_small(u, lines):
    size = len(lines)
    lower, inverse = {}, []
    solved = []
    scale = reciprocal(u[0, 0])
    for j in range(size):
        inverse.append(scale)
        if j + 1 < size:
            pivot = u[j + 1, j + 1] - (u[j, j + 1] * u[j, j + 1]) * scale
        for i in range(j + 1, size):
            lower[i, j] = u[j, i] * scale
        if j + 1 < size:
            scale = reciprocal(pivot)
        for i in range(j + 1, size):
            for m in range(i, size):
                if m > j + 1:
                    u[i, m] = u[i, m] - lower[i, j] * u[j, m]
        solved.append(lines[j])
        for i in range(j + 1, size):
            lines[i] = [x - lower[i, j] * y for x, y in zip(lines[i], lines[j])]
    for j in reversed(range(size)):
        solved[j] = [x * inverse[j] for x in solved[j]]
        for i in range(j + 1, size):
            solved[j] = [x - lower[i, j] * y for x, y in zip(solved[j], solved[i])]
    return solved


def tree_sum(terms):
    while len(terms) > 1:
        terms = [a + b for a, b in zip(terms[::2], terms[1::2])]
    return terms[0]


def panel_sweep(groups, first):
    sub_ids = lax.broadcasted_iota(jnp.int32, (SUB, LANES), 0)
    lane_ids = lax.broadcasted_iota(jnp.int32, (SUB, LANES), 1)
    for p in range(len(groups)):
        tile, lane = divmod(first + p * SUB, LANES)
        pivot_lanes = (lane_ids // SUB) == lane // SUB
        spread = [lane_of(groups[p][tile], lane + j) for j in range(SUB)]
        u = {(i, j): row_of(spread[j], i) for j in range(SUB) for i in range(j + 1)}
        sources = []
        for j in range(SUB):
            line = [row_of(x, j) for x in groups[p]]
            line[tile] = jnp.where(
                pivot_lanes, jnp.where(lane_ids == lane + j, -1.0, 0.0), line[tile]
            )
            sources.append(line)
        tiles = range(len(groups[p]))
        lines = solve_small(u, sources)
        for g in range(len(groups)):
            if g == p:
                continue
            factors = [lane_of(groups[g][tile], lane + j) for j in range(SUB)]
            for t in tiles:
                kept = groups[g][t]
                if t == tile:
                    kept = jnp.where(pivot_lanes, 0.0, kept)
                groups[g][t] = kept - tree_sum([factors[j] * lines[j][t] for j in range(SUB)])
        for t in tiles:
            row = lines[0][t]
            for j in range(1, SUB):
                row = jnp.where(sub_ids == j, lines[j][t], row)
            groups[p][t] = row
    return groups


def block_sweep(d_ref):
    wide = d_ref.shape[0]
    lane_ids = lax.broadcasted_iota(jnp.int32, (wide, wide), 1)
    for first in range(0, wide, BASE):
        old = d_ref[first : first + BASE, :]
        groups = [
            [old[g : g + SUB, t : t + LANES] for t in range(0, wide, LANES)]
            for g in range(0, BASE, SUB)
        ]
        groups = panel_sweep(groups, first)
        new = jnp.concatenate([jnp.concatenate(g, axis=1) for g in groups], axis=0)
        update = lax.dot_general(
            stacked(old, LEFT, 0),
            stacked(new, RIGHT, 0),
            (((0,), (0,)), ((), ())),
            preferred_element_type=jnp.float32,
        )
        kept = jnp.where(lane_ids // BASE == first // BASE, 0.0, d_ref[...])
        d_ref[...] = kept - update
        d_ref[first : first + BASE, :] = new


def invert_kernel(
    scalar_ref, traces_ref, rows_hbm, one_hbm, two_hbm, three_hbm,
    band_hbm, full_ref, m_ref, d_ref, left_ref, right_ref, band_ref, in_sems, out_sem,
):
    wide, n = rows_hbm.shape
    count = n // wide
    mp_index = scalar_ref[1]

    def block(i):
        return slice(i * wide, (i + 1) * wide)

    def place(i):
        return pl.ds(pl.multiple_of(lax.rem(mp_index + i, count) * wide, wide), wide)

    @pl.when(scalar_ref[0] > 0)
    def _():
        arrivals = [(rows_hbm.at[:, place(j)], 0, j) for j in range(count)]
        for i, source in enumerate((one_hbm, two_hbm, three_hbm)):
            arrivals.append((source.at[:, block(0)], i + 1, i + 1))
            arrivals.append((source.at[:, block(1)], i + 1, (i + 1) % (count - 1) + 1))
        copies = [
            pltpu.make_async_copy(source, m_ref.at[block(i), block(j)], in_sems.at[at])
            for at, (source, i, j) in enumerate(arrivals)
        ]
        for copy in copies:
            copy.start()

        traces = jnp.sum(traces_ref[...], axis=0, keepdims=True)
        lane_ids = lax.broadcasted_iota(jnp.int32, traces.shape, 1)

        def pick_lane(lane):
            return jnp.sum(jnp.where(lane_ids == lane, traces, 0.0), axis=1, keepdims=True)

        lane = 2 * scalar_ref[2]
        ratio = jnp.sqrt(pick_lane(lane) / FF / (pick_lane(lane + 1) / D))
        shift = jnp.where(scalar_ref[3] > 0, DAMPING_BASE * ratio, DAMPING_BASE / ratio)
        diagonal = lax.broadcasted_iota(jnp.int32, (wide, wide), 0) == lax.broadcasted_iota(
            jnp.int32, (wide, wide), 1
        )
        for copy in copies:
            copy.wait()

        for _, i, j in arrivals:
            value = m_ref[block(i), block(j)]
            if i == j:
                m_ref[block(i), block(i)] = jnp.where(diagonal, value + shift, value)
            else:
                m_ref[block(j), block(i)] = value.T

        @pl.loop(0, count)
        def _(k):
            at = pl.ds(pl.multiple_of(k * wide, wide), wide)
            d_ref[...] = m_ref[at, at]
            block_sweep(d_ref)

            left_ref[...] = stacked(m_ref[:, at], LEFT, 1)
            right_ref[...] = stacked(m_ref[at, :], RIGHT, 0)
            rows = -dot(stacked(d_ref[...], LEFT, 1), right_ref[...])
            m_ref[:, at] = jnp.zeros((n, wide), jnp.float32)
            m_ref[at, :] = rows
            m_ref[at, at] = d_ref[...]
            right_ref[...] = stacked(m_ref[at, :], RIGHT, 0)
            for i in range(count):

                @pl.when(i != k)
                def _():
                    m_ref[block(i), :] = m_ref[block(i), :] - dot(left_ref[block(i), :], right_ref[...])

        for j in range(count):
            band = (-m_ref[block(0), block(j)]).astype(jnp.bfloat16)
            for r in range(wide // ROWS):
                for c in range(wide // LANES):
                    at = lax.rem(mp_index + j, count) * (wide // LANES) + r * (n // LANES) + c
                    band_ref[at] = band[r * ROWS : (r + 1) * ROWS, c * LANES : (c + 1) * LANES]
        sent = pltpu.make_async_copy(band_ref, band_hbm, out_sem)
        sent.start()
        for j in range(count):
            for i in range(count):
                full_ref[place(i), place(j)] = (-m_ref[block(i), block(j)]).astype(jnp.bfloat16)
        sent.wait()

    @pl.when(scalar_ref[0] <= 0)
    def _():
        band_ref[...] = jnp.zeros(band_ref.shape, jnp.bfloat16)
        full_ref[...] = jnp.zeros(full_ref.shape, jnp.bfloat16)
        sent = pltpu.make_async_copy(band_ref, band_hbm, out_sem)
        sent.start()
        sent.wait()


def invert(scalars, traces, rows, one, two, three):
    wide, n = rows.shape
    in_smem = pl.BlockSpec(memory_space=pltpu.SMEM)
    in_vmem = pl.BlockSpec(memory_space=pltpu.VMEM)
    in_hbm = pl.BlockSpec(memory_space=pltpu.HBM)
    pieces = (wide * n // (ROWS * LANES), ROWS, LANES)
    return pl.pallas_call(
        invert_kernel,
        out_shape=(
            jax.ShapeDtypeStruct(pieces, jnp.bfloat16),
            jax.ShapeDtypeStruct((n, n), jnp.bfloat16),
        ),
        in_specs=[in_smem, in_vmem] + [in_hbm] * 4,
        out_specs=(in_hbm, in_vmem),
        scratch_shapes=[
            pltpu.VMEM((n, n), jnp.float32),
            pltpu.VMEM((wide, wide), jnp.float32),
            pltpu.VMEM((n, 3 * wide), jnp.bfloat16),
            pltpu.VMEM((3 * wide, n), jnp.bfloat16),
            pltpu.VMEM(pieces, jnp.bfloat16),
            pltpu.SemaphoreType.DMA((10,)),
            pltpu.SemaphoreType.DMA,
        ],
        compiler_params=pltpu.CompilerParams(vmem_limit_bytes=56 * 1024 * 1024),
        cost_estimate=pl.CostEstimate(
            flops=36 * n * n * n, bytes_accessed=6 * n * n, transcendentals=0
        ),
    )(scalars, traces, rows, one, two, three)


def prepare_kernel(mp_ref, rows_ref, near_ref, far_ref, trace_ref):
    wide, n = rows_ref.shape

    def place(i):
        return pl.ds(pl.multiple_of(lax.rem(mp_ref[0] + i, n // wide) * wide, wide), wide)

    own = rows_ref[:, place(0)]
    diagonal = lax.broadcasted_iota(jnp.int32, own.shape, 0) == lax.broadcasted_iota(
        jnp.int32, own.shape, 1
    )
    trace = jnp.sum(jnp.where(diagonal, own, 0.0), axis=0, keepdims=True)
    trace = jnp.sum(trace, axis=1, keepdims=True)
    trace_ref[...] = jnp.broadcast_to(trace[None], trace_ref.shape)
    near_ref[:, :wide] = own
    near_ref[:, wide:] = rows_ref[:, place(1)]
    far_ref[:, :wide] = own
    far_ref[:, wide:] = rows_ref[:, place(2)]


def prepare(mp_index, rows, copies):
    wide, n = rows.shape
    in_vmem = pl.BlockSpec(memory_space=pltpu.VMEM)
    return pl.pallas_call(
        prepare_kernel,
        out_shape=(
            jax.ShapeDtypeStruct((wide, 2 * wide), jnp.float32),
            jax.ShapeDtypeStruct((wide, 2 * wide), jnp.float32),
            jax.ShapeDtypeStruct((copies, 1, LANES), jnp.float32),
        ),
        in_specs=[pl.BlockSpec(memory_space=pltpu.SMEM), in_vmem],
        out_specs=(in_vmem,) * 3,
        compiler_params=pltpu.CompilerParams(vmem_limit_bytes=8 * 1024 * 1024),
    )(mp_index.reshape(1).astype(jnp.int32), rows)


def pick_kernel(index_ref, src_ref, out_ref):
    @pl.loop(0, out_ref.shape[0], unroll=8)
    def _(i):
        out_ref[i] = src_ref[index_ref[i]]


def pick(index, source):
    in_vmem = pl.BlockSpec(memory_space=pltpu.VMEM)
    return pl.pallas_call(
        pick_kernel,
        out_shape=jax.ShapeDtypeStruct(index.shape + source.shape[1:], source.dtype),
        in_specs=[pl.BlockSpec(memory_space=pltpu.SMEM), in_vmem],
        out_specs=in_vmem,
        compiler_params=pltpu.CompilerParams(vmem_limit_bytes=4 * 1024 * 1024),
    )(index, source)


def take(source, index):
    return source.at[index].get(mode="promise_in_bounds")


def positions(slot_ids, wanted):
    slot_range = jnp.arange(slot_ids.shape[0], dtype=jnp.int32)
    hit = slot_ids[None, :] == wanted[:, None]
    return jnp.sum(jnp.where(hit, slot_range[None, :], 0), axis=1).astype(jnp.int32)


def exchange(pieces, axes):
    return lax.all_to_all(pieces, axes, split_axis=0, concat_axis=0, tiled=True)


def from_ahead(value, axis, step):
    count = lax.axis_size(axis)
    return lax.ppermute(value, axis, [((i + step) % count, i) for i in range(count)])


def local(old_factors, gradients, old_slots, new_slots):
    mp_index = lax.axis_index("mp")
    mp_count = lax.axis_size("mp")
    z_count, x_count, c_count = lax.axis_size("z"), lax.axis_size("x"), lax.axis_size("c")
    z, x, c = lax.axis_index("z"), lax.axis_index("x"), lax.axis_index("c")
    dp_count = z_count * x_count * c_count
    dp_index = (z * x_count + x) * c_count + c
    band, width = old_factors.shape[2:]
    tile_count, row_count = gradients.shape[1:3]
    a_span = FF // width
    layer_blocks = a_span + D // width
    layers = tile_count // a_span
    old_flat = old_slots.reshape(dp_count)
    new_flat = new_slots.reshape(dp_count)
    own = lax.dynamic_index_in_dim(old_flat, dp_index, keepdims=False)
    own_block = jnp.maximum(own, 0)
    own_layer = own_block // layer_blocks
    own_input = own_block % layer_blocks < a_span

    rows = old_factors[0, 0]
    near, far, trace = prepare(mp_index, rows, x_count * c_count * mp_count)
    trace = exchange(trace, ("x", "c", "mp")).reshape(x_count * c_count, mp_count, LANES)
    plane = lax.dynamic_slice_in_dim(old_flat, z * x_count * c_count, x_count * c_count)
    plane_bin = 2 * (plane // layer_blocks) + jnp.where(plane % layer_blocks < a_span, 0, 1)
    plane_bin = jnp.where(plane >= 0, plane_bin, -1)
    lane_ids = lax.broadcasted_iota(jnp.int32, (1, 1, LANES), 2)
    binned = jnp.sum(jnp.where(lane_ids == plane_bin[:, None, None], trace, 0.0), axis=(0, 1))
    binned, tiles = lax.optimization_barrier((binned, gradients[0]))
    binned = jnp.broadcast_to(binned[None, None], (z_count, 1, LANES))
    traces = exchange(binned, "z").reshape(z_count, LANES)
    traces, near, far = lax.optimization_barrier((traces, near, far))

    one = from_ahead(near, "mp", 1)
    two = from_ahead(near, "mp", 2)
    three = from_ahead(far, "mp", 3)

    block = jnp.maximum(old_flat, 0)
    tile_of = jnp.minimum(block // layer_blocks * a_span + block % layer_blocks, tile_count - 1)
    tile_of = tile_of.reshape(z_count * x_count, c_count)

    def tiles_of(core):
        return take(tiles, lax.dynamic_index_in_dim(tile_of, core, 1, keepdims=False))

    arrived = from_ahead(tiles_of(1 - c), "c", 1)
    partial = tiles_of(c).astype(jnp.float32) + arrived.astype(jnp.float32)
    partial, traces = lax.optimization_barrier((partial.astype(jnp.bfloat16), traces))
    partial = exchange(partial, ("z", "x"))
    tile = jnp.sum(partial.astype(jnp.float32), axis=0).astype(jnp.bfloat16)

    scalars = jnp.stack(
        [v.astype(jnp.int32) for v in (own >= 0, mp_index, own_layer, own_input)]
    )
    inverse_band, inverse = invert(scalars, traces, rows, one, two, three)
    inverse_band, tile = lax.optimization_barrier((inverse_band, tile))

    def gather(value, axis, steps):
        return jnp.stack([value] + [from_ahead(value, axis, step) for step in steps])

    held = jnp.dot(tile, inverse, preferred_element_type=jnp.float32).astype(jnp.bfloat16)
    held = lax.all_gather(held, "z", axis=0, tiled=False)
    spread = exchange(inverse_band, DP)
    slot_range = jnp.arange(dp_count, dtype=jnp.int32)
    empty = jnp.min(jnp.where(old_flat >= 0, dp_count - 1, slot_range))
    source = jnp.where(new_flat >= 0, positions(old_flat, new_flat), empty)
    outgoing, held = lax.optimization_barrier((pick(source, spread), held))
    arrived = exchange(outgoing, DP)
    arrived = arrived.reshape(band // ROWS, width // LANES, ROWS, LANES)
    inverses = arrived.transpose(0, 2, 1, 3).reshape(1, 1, band, width)
    held = gather(gather(held, "x", (1, 2, 3)), "c", (1,))
    held = held.reshape(dp_count, row_count, width)
    tile_range = jnp.arange(tile_count, dtype=jnp.int32)
    place = positions(old_flat, tile_range // a_span * layer_blocks + tile_range % a_span)
    far_x = (place // c_count - x + x_count) % x_count
    far_c = (place - c + c_count) % c_count
    from_z = place // (x_count * c_count)
    precond = take(held, (far_c * x_count + far_x) * z_count + from_z)
    return (inverses, precond)


def solution(mesh):
    dp_count, mp_count = mesh.devices.shape
    z_count = dp_count // (X_COUNT * CORES)
    parts = Mesh(
        mesh.devices.reshape(z_count, X_COUNT, CORES, mp_count), DP + ("mp",)
    )
    in_specs = (P(DP, None, "mp", None), P(DP, None, "mp", None), P(), P())
    out_specs = (P(DP, None, "mp", None), P(None, "mp", None))
    return jax.shard_map(local, mesh=parts, in_specs=in_specs, out_specs=out_specs, check_vma=False)
```

```python
import jax
import jax.numpy as jnp
from jax import lax
from jax.experimental import pallas as pl
from jax.experimental.pallas import tpu as pltpu
from jax.sharding import Mesh, PartitionSpec as P

D = 8192
FF = 28672
DAMPING_BASE = 2.0
X_COUNT, CORES = 4, 2
DP = ("z", "x", "c")

BASE = 32
SUB = 8
ROWS, LANES = 16, 128


def row_of(x, j):
    return jnp.broadcast_to(x[j : j + 1, :], x.shape)


def lane_of(x, j):
    return jnp.broadcast_to(x[:, j : j + 1], x.shape)


def reciprocal(x):
    return pltpu.reciprocal(x, approx=True)


def halves(x):
    high = x.astype(jnp.bfloat16)
    return high, (x - high.astype(jnp.float32)).astype(jnp.bfloat16)


def stacked(x, order, axis):
    parts = halves(x)
    return jnp.concatenate([parts[i] for i in order], axis=axis)


LEFT, RIGHT = (0, 0, 1), (0, 1, 0)


def dot(left, right):
    return jnp.dot(left, right, preferred_element_type=jnp.float32)


def panel_sweep(groups, first):
    sub_ids = lax.broadcasted_iota(jnp.int32, (SUB, LANES), 0)
    lane_ids = lax.broadcasted_iota(jnp.int32, (SUB, LANES), 1)
    for p in range(len(groups)):
        tile, lane = divmod(first + p * SUB, LANES)
        pivot_lanes = (lane_ids // SUB) == lane // SUB
        spread = [lane_of(groups[p][tile], lane + j) for j in range(SUB)]
        rows = list(groups[p])
        rows[tile] = jnp.where(
            pivot_lanes, jnp.where(lane_ids == sub_ids + lane, 1.0, 0.0), rows[tile]
        )
        pivot = row_of(spread[0], 0)
        for j in range(SUB):
            here = sub_ids == j
            scale = reciprocal(pivot)
            if j + 1 < SUB:
                cross = row_of(spread[j], j + 1) * row_of(spread[j + 1], j)
                pivot = row_of(spread[j + 1], j + 1) - cross * scale
            column = jnp.where(here, -1.0, spread[j])

            def eliminate(x):
                line = row_of(x, j)
                return jnp.where(here, 0.0, x) - (column * line) * scale

            rows = [eliminate(x) for x in rows]
            for i in range(j + 1, SUB):
                spread[i] = eliminate(spread[i])
        rows[tile] = jnp.where(pivot_lanes, -rows[tile], rows[tile])
        lines = [[row_of(x, j) for x in rows] for j in range(SUB)]
        for g in range(len(groups)):
            if g == p:
                continue
            factors = [lane_of(groups[g][tile], lane + j) for j in range(SUB)]
            for t in range(len(rows)):
                terms = [factors[j] * lines[j][t] for j in range(SUB)]
                while len(terms) > 1:
                    terms = [a + b for a, b in zip(terms[::2], terms[1::2])]
                kept = groups[g][t]
                if t == tile:
                    kept = jnp.where(pivot_lanes, 0.0, kept)
                groups[g][t] = kept - terms[0]
        groups[p] = rows
    return groups


def block_sweep(d_ref):
    wide = d_ref.shape[0]
    lane_ids = lax.broadcasted_iota(jnp.int32, (wide, wide), 1)
    for first in range(0, wide, BASE):
        old = d_ref[first : first + BASE, :]
        groups = [
            [old[g : g + SUB, t : t + LANES] for t in range(0, wide, LANES)]
            for g in range(0, BASE, SUB)
        ]
        groups = panel_sweep(groups, first)
        new = jnp.concatenate([jnp.concatenate(g, axis=1) for g in groups], axis=0)
        update = lax.dot_general(
            stacked(old, LEFT, 0),
            stacked(new, RIGHT, 0),
            (((0,), (0,)), ((), ())),
            preferred_element_type=jnp.float32,
        )
        kept = jnp.where(lane_ids // BASE == first // BASE, 0.0, d_ref[...])
        d_ref[...] = kept - update
        d_ref[first : first + BASE, :] = new


def invert_kernel(
    slots_ref, traces_ref, rows_hbm, one_hbm, two_hbm, three_hbm,
    band_hbm, full_ref, m_ref, d_ref, left_ref, right_ref, band_ref, in_sems, out_sem,
):
    wide, n = rows_hbm.shape
    count = n // wide
    dp_index, mp_index = slots_ref[slots_ref.shape[0] - 2], slots_ref[slots_ref.shape[0] - 1]
    own = slots_ref[dp_index]
    a_span = FF // n
    layer_blocks = a_span + D // n
    layer = lax.div(own, layer_blocks)

    def block(i):
        return slice(i * wide, (i + 1) * wide)

    def place(i):
        return pl.ds(pl.multiple_of(lax.rem(mp_index + i, count) * wide, wide), wide)

    @pl.when(own >= 0)
    def _():
        arrivals = [(rows_hbm.at[:, place(j)], 0, j) for j in range(count)]
        for i, source in enumerate((one_hbm, two_hbm, three_hbm)):
            arrivals.append((source.at[:, block(0)], i + 1, i + 1))
            arrivals.append((source.at[:, block(1)], i + 1, (i + 1) % (count - 1) + 1))
        copies = [
            pltpu.make_async_copy(source, m_ref.at[block(i), block(j)], in_sems.at[at])
            for at, (source, i, j) in enumerate(arrivals)
        ]
        for copy in copies:
            copy.start()

        traces = jnp.sum(traces_ref[...], axis=0, keepdims=True)
        lane_ids = lax.broadcasted_iota(jnp.int32, traces.shape, 1)

        def pick_lane(lane):
            return jnp.sum(jnp.where(lane_ids == lane, traces, 0.0), axis=1, keepdims=True)

        lane = 2 * layer
        ratio = jnp.sqrt(pick_lane(lane) / FF / (pick_lane(lane + 1) / D))
        shift = jnp.where(lax.rem(own, layer_blocks) < a_span, DAMPING_BASE * ratio, DAMPING_BASE / ratio)
        diagonal = lax.broadcasted_iota(jnp.int32, (wide, wide), 0) == lax.broadcasted_iota(
            jnp.int32, (wide, wide), 1
        )
        for copy in copies:
            copy.wait()

        for _, i, j in arrivals:
            value = m_ref[block(i), block(j)]
            if i == j:
                m_ref[block(i), block(i)] = jnp.where(diagonal, value + shift, value)
            else:
                m_ref[block(j), block(i)] = value.T

        @pl.loop(0, count)
        def _(k):
            at = pl.ds(pl.multiple_of(k * wide, wide), wide)
            d_ref[...] = m_ref[at, at]
            block_sweep(d_ref)

            left_ref[...] = stacked(m_ref[:, at], LEFT, 1)
            right_ref[...] = stacked(m_ref[at, :], RIGHT, 0)
            rows = -dot(stacked(d_ref[...], LEFT, 1), right_ref[...])
            m_ref[:, at] = jnp.zeros((n, wide), jnp.float32)
            m_ref[at, :] = rows
            m_ref[at, at] = d_ref[...]
            right_ref[...] = stacked(m_ref[at, :], RIGHT, 0)
            for i in range(count):

                @pl.when(i != k)
                def _():
                    m_ref[block(i), :] = m_ref[block(i), :] - dot(left_ref[block(i), :], right_ref[...])

        for j in range(count):
            band = (-m_ref[block(0), block(j)]).astype(jnp.bfloat16)
            for r in range(wide // ROWS):
                for c in range(wide // LANES):
                    at = lax.rem(mp_index + j, count) * (wide // LANES) + r * (n // LANES) + c
                    band_ref[at] = band[r * ROWS : (r + 1) * ROWS, c * LANES : (c + 1) * LANES]
        sent = pltpu.make_async_copy(band_ref, band_hbm, out_sem)
        sent.start()
        for j in range(count):
            for i in range(count):
                full_ref[place(i), place(j)] = (-m_ref[block(i), block(j)]).astype(jnp.bfloat16)
        sent.wait()

    @pl.when(own < 0)
    def _():
        band_ref[...] = jnp.zeros(band_ref.shape, jnp.bfloat16)
        full_ref[...] = jnp.zeros(full_ref.shape, jnp.bfloat16)
        sent = pltpu.make_async_copy(band_ref, band_hbm, out_sem)
        sent.start()
        sent.wait()


def invert(slots, traces, rows, one, two, three):
    wide, n = rows.shape
    in_smem = pl.BlockSpec(memory_space=pltpu.SMEM)
    in_vmem = pl.BlockSpec(memory_space=pltpu.VMEM)
    in_hbm = pl.BlockSpec(memory_space=pltpu.HBM)
    pieces = (wide * n // (ROWS * LANES), ROWS, LANES)
    return pl.pallas_call(
        invert_kernel,
        out_shape=(
            jax.ShapeDtypeStruct(pieces, jnp.bfloat16),
            jax.ShapeDtypeStruct((n, n), jnp.bfloat16),
        ),
        in_specs=[in_smem, in_vmem] + [in_hbm] * 4,
        out_specs=(in_hbm, in_vmem),
        scratch_shapes=[
            pltpu.VMEM((n, n), jnp.float32),
            pltpu.VMEM((wide, wide), jnp.float32),
            pltpu.VMEM((n, 3 * wide), jnp.bfloat16),
            pltpu.VMEM((3 * wide, n), jnp.bfloat16),
            pltpu.VMEM(pieces, jnp.bfloat16),
            pltpu.SemaphoreType.DMA((10,)),
            pltpu.SemaphoreType.DMA,
        ],
        compiler_params=pltpu.CompilerParams(vmem_limit_bytes=56 * 1024 * 1024),
        cost_estimate=pl.CostEstimate(
            flops=36 * n * n * n, bytes_accessed=6 * n * n, transcendentals=0
        ),
    )(slots, traces, rows, one, two, three)


def prepare_kernel(mp_ref, rows_ref, near_ref, far_ref, trace_ref):
    wide, n = rows_ref.shape

    def place(i):
        return pl.ds(pl.multiple_of(lax.rem(mp_ref[0] + i, n // wide) * wide, wide), wide)

    own = rows_ref[:, place(0)]
    diagonal = lax.broadcasted_iota(jnp.int32, own.shape, 0) == lax.broadcasted_iota(
        jnp.int32, own.shape, 1
    )
    trace = jnp.sum(jnp.where(diagonal, own, 0.0), axis=0, keepdims=True)
    trace = jnp.sum(trace, axis=1, keepdims=True)
    trace_ref[...] = jnp.broadcast_to(trace[None], trace_ref.shape)
    near_ref[:, :wide] = own
    near_ref[:, wide:] = rows_ref[:, place(1)]
    far_ref[:, :wide] = own
    far_ref[:, wide:] = rows_ref[:, place(2)]


def prepare(mp_index, rows, copies):
    wide, n = rows.shape
    in_vmem = pl.BlockSpec(memory_space=pltpu.VMEM)
    return pl.pallas_call(
        prepare_kernel,
        out_shape=(
            jax.ShapeDtypeStruct((wide, 2 * wide), jnp.float32),
            jax.ShapeDtypeStruct((wide, 2 * wide), jnp.float32),
            jax.ShapeDtypeStruct((copies, 1, LANES), jnp.float32),
        ),
        in_specs=[pl.BlockSpec(memory_space=pltpu.SMEM), in_vmem],
        out_specs=(in_vmem,) * 3,
        compiler_params=pltpu.CompilerParams(vmem_limit_bytes=8 * 1024 * 1024),
    )(mp_index.reshape(1).astype(jnp.int32), rows)


def pick_kernel(index_ref, src_ref, out_ref):
    @pl.loop(0, out_ref.shape[0], unroll=8)
    def _(i):
        out_ref[i] = src_ref[index_ref[i]]


def pick(index, source):
    in_vmem = pl.BlockSpec(memory_space=pltpu.VMEM)
    return pl.pallas_call(
        pick_kernel,
        out_shape=jax.ShapeDtypeStruct(index.shape + source.shape[1:], source.dtype),
        in_specs=[pl.BlockSpec(memory_space=pltpu.SMEM), in_vmem],
        out_specs=in_vmem,
        compiler_params=pltpu.CompilerParams(vmem_limit_bytes=4 * 1024 * 1024),
    )(index, source)


def take(source, index):
    return source.at[index].get(mode="promise_in_bounds")


def positions(slot_ids, wanted):
    slot_range = jnp.arange(slot_ids.shape[0], dtype=jnp.int32)
    hit = slot_ids[None, :] == wanted[:, None]
    return jnp.sum(jnp.where(hit, slot_range[None, :], 0), axis=1).astype(jnp.int32)


def exchange(pieces, axes):
    return lax.all_to_all(pieces, axes, split_axis=0, concat_axis=0, tiled=True)


def from_ahead(value, axis, step):
    count = lax.axis_size(axis)
    return lax.ppermute(value, axis, [((i + step) % count, i) for i in range(count)])


def local(old_factors, gradients, old_slots, new_slots):
    mp_index = lax.axis_index("mp")
    mp_count = lax.axis_size("mp")
    z_count, x_count, c_count = lax.axis_size("z"), lax.axis_size("x"), lax.axis_size("c")
    z, x, c = lax.axis_index("z"), lax.axis_index("x"), lax.axis_index("c")
    dp_count = z_count * x_count * c_count
    dp_index = (z * x_count + x) * c_count + c
    band, width = old_factors.shape[2:]
    tile_count, row_count = gradients.shape[1:3]
    a_span = FF // width
    layer_blocks = a_span + D // width
    old_flat = old_slots.reshape(dp_count)
    new_flat = new_slots.reshape(dp_count)

    rows = old_factors[0, 0]
    near, far, trace = prepare(mp_index, rows, x_count * c_count * mp_count)
    trace = exchange(trace, ("x", "c", "mp")).reshape(x_count * c_count, mp_count, LANES)
    plane = lax.dynamic_slice_in_dim(old_flat, z * x_count * c_count, x_count * c_count)
    plane_bin = 2 * (plane // layer_blocks) + jnp.where(plane % layer_blocks < a_span, 0, 1)
    plane_bin = jnp.where(plane >= 0, plane_bin, -1)
    lane_ids = lax.broadcasted_iota(jnp.int32, (1, 1, LANES), 2)
    binned = jnp.sum(jnp.where(lane_ids == plane_bin[:, None, None], trace, 0.0), axis=(0, 1))
    binned, near, far, tiles = lax.optimization_barrier((binned, near, far, gradients[0]))
    binned = jnp.broadcast_to(binned[None, None], (z_count, 1, LANES))
    traces = exchange(binned, "z").reshape(z_count, LANES)

    one = from_ahead(near, "mp", 1)
    two = from_ahead(near, "mp", 2)
    three = from_ahead(far, "mp", 3)

    block = jnp.maximum(old_flat, 0)
    tile_of = jnp.minimum(block // layer_blocks * a_span + block % layer_blocks, tile_count - 1)
    tile_of = tile_of.reshape(z_count * x_count, c_count)

    def tiles_of(core):
        return take(tiles, lax.dynamic_index_in_dim(tile_of, core, 1, keepdims=False))

    arrived = from_ahead(tiles_of(1 - c), "c", 1)
    partial = tiles_of(c).astype(jnp.float32) + arrived.astype(jnp.float32)
    partial, traces = lax.optimization_barrier((partial.astype(jnp.bfloat16), traces))
    partial = exchange(partial, ("z", "x"))
    tile = jnp.sum(partial.astype(jnp.float32), axis=0).astype(jnp.bfloat16)

    places = jnp.stack([dp_index.astype(jnp.int32), mp_index.astype(jnp.int32)])
    slots = jnp.concatenate([old_flat, places])
    inverse_band, inverse = invert(slots, traces, rows, one, two, three)
    inverse_band, tile = lax.optimization_barrier((inverse_band, tile))

    def gather(value, axis, steps):
        return jnp.stack([value] + [from_ahead(value, axis, step) for step in steps])

    held = jnp.dot(tile, inverse, preferred_element_type=jnp.float32).astype(jnp.bfloat16)
    held = lax.all_gather(held, "z", axis=0, tiled=False)
    spread = exchange(inverse_band, DP)
    slot_range = jnp.arange(dp_count, dtype=jnp.int32)
    empty = jnp.min(jnp.where(old_flat >= 0, dp_count - 1, slot_range))
    source = jnp.where(new_flat >= 0, positions(old_flat, new_flat), empty)
    outgoing, held = lax.optimization_barrier((pick(source, spread), held))
    arrived = exchange(outgoing, DP)
    arrived = arrived.reshape(band // ROWS, width // LANES, ROWS, LANES)
    inverses = arrived.transpose(0, 2, 1, 3).reshape(1, 1, band, width)
    held = gather(gather(held, "x", (1, 2, 3)), "c", (1,))
    held = held.reshape(dp_count, row_count, width)
    tile_range = jnp.arange(tile_count, dtype=jnp.int32)
    place = positions(old_flat, tile_range // a_span * layer_blocks + tile_range % a_span)
    far_x = (place // c_count - x + x_count) % x_count
    far_c = (place - c + c_count) % c_count
    from_z = place // (x_count * c_count)
    precond = take(held, (far_c * x_count + far_x) * z_count + from_z)
    return (inverses, precond)


def solution(mesh):
    dp_count, mp_count = mesh.devices.shape
    z_count = dp_count // (X_COUNT * CORES)
    parts = Mesh(
        mesh.devices.reshape(z_count, X_COUNT, CORES, mp_count), DP + ("mp",)
    )
    in_specs = (P(DP, None, "mp", None), P(DP, None, "mp", None), P(), P())
    out_specs = (P(DP, None, "mp", None), P(None, "mp", None))
    return jax.shard_map(local, mesh=parts, in_specs=in_specs, out_specs=out_specs, check_vma=False)
```

```python
import jax
import jax.numpy as jnp
from jax import lax
from jax.experimental import pallas as pl
from jax.experimental.pallas import tpu as pltpu
from jax.sharding import Mesh, PartitionSpec as P

D = 8192
FF = 28672
DAMPING_BASE = 2.0
X_COUNT, CORES = 4, 2
DP = ("z", "x", "c")

BASE = 32
SUB = 8
ROWS, LANES = 16, 128


def row_of(x, j):
    return jnp.broadcast_to(x[j : j + 1, :], x.shape)


def lane_of(x, j):
    return jnp.broadcast_to(x[:, j : j + 1], x.shape)


def reciprocal(x):
    return pltpu.reciprocal(x, approx=True)


def halves(x):
    high = x.astype(jnp.bfloat16)
    return high, (x - high.astype(jnp.float32)).astype(jnp.bfloat16)


def stacked(x, order, axis):
    parts = halves(x)
    return jnp.concatenate([parts[i] for i in order], axis=axis)


LEFT, RIGHT = (0, 0, 1), (0, 1, 0)


def dot(left, right):
    return jnp.dot(left, right, preferred_element_type=jnp.float32)


def panel_sweep(groups, first):
    sub_ids = lax.broadcasted_iota(jnp.int32, (SUB, LANES), 0)
    lane_ids = lax.broadcasted_iota(jnp.int32, (SUB, LANES), 1)
    for p in range(len(groups)):
        tile, lane = divmod(first + p * SUB, LANES)
        pivot_lanes = (lane_ids // SUB) == lane // SUB
        spread = [lane_of(groups[p][tile], lane + j) for j in range(SUB)]
        rows = list(groups[p])
        rows[tile] = jnp.where(
            pivot_lanes, jnp.where(lane_ids == sub_ids + lane, 1.0, 0.0), rows[tile]
        )
        pivot = row_of(spread[0], 0)
        for j in range(SUB):
            here = sub_ids == j
            scale = reciprocal(pivot)
            if j + 1 < SUB:
                cross = row_of(spread[j], j + 1) * row_of(spread[j + 1], j)
                pivot = row_of(spread[j + 1], j + 1) - cross * scale
            column = jnp.where(here, -1.0, spread[j])

            def eliminate(x):
                line = row_of(x, j)
                return jnp.where(here, 0.0, x) - (column * line) * scale

            rows = [eliminate(x) for x in rows]
            for i in range(j + 1, SUB):
                spread[i] = eliminate(spread[i])
        rows[tile] = jnp.where(pivot_lanes, -rows[tile], rows[tile])
        lines = [[row_of(x, j) for x in rows] for j in range(SUB)]
        for g in range(len(groups)):
            if g == p:
                continue
            factors = [lane_of(groups[g][tile], lane + j) for j in range(SUB)]
            for t in range(len(rows)):
                terms = [factors[j] * lines[j][t] for j in range(SUB)]
                while len(terms) > 1:
                    terms = [a + b for a, b in zip(terms[::2], terms[1::2])]
                kept = groups[g][t]
                if t == tile:
                    kept = jnp.where(pivot_lanes, 0.0, kept)
                groups[g][t] = kept - terms[0]
        groups[p] = rows
    return groups


def block_sweep(d_ref):
    wide = d_ref.shape[0]
    lane_ids = lax.broadcasted_iota(jnp.int32, (wide, wide), 1)
    for first in range(0, wide, BASE):
        old = d_ref[first : first + BASE, :]
        groups = [
            [old[g : g + SUB, t : t + LANES] for t in range(0, wide, LANES)]
            for g in range(0, BASE, SUB)
        ]
        groups = panel_sweep(groups, first)
        new = jnp.concatenate([jnp.concatenate(g, axis=1) for g in groups], axis=0)
        update = lax.dot_general(
            stacked(old, LEFT, 0),
            stacked(new, RIGHT, 0),
            (((0,), (0,)), ((), ())),
            preferred_element_type=jnp.float32,
        )
        kept = jnp.where(lane_ids // BASE == first // BASE, 0.0, d_ref[...])
        d_ref[...] = kept - update
        d_ref[first : first + BASE, :] = new


def invert_kernel(
    slots_ref, traces_ref, rows_hbm, one_hbm, two_hbm, three_hbm,
    band_hbm, full_ref, m_ref, d_ref, left_ref, right_ref, band_ref, in_sems, out_sem,
):
    wide, n = rows_hbm.shape
    count = n // wide
    dp_index, mp_index = slots_ref[slots_ref.shape[0] - 2], slots_ref[slots_ref.shape[0] - 1]
    own = slots_ref[dp_index]
    a_span = FF // n
    layer_blocks = a_span + D // n
    layer = lax.div(own, layer_blocks)

    def block(i):
        return slice(i * wide, (i + 1) * wide)

    def place(i):
        return pl.ds(pl.multiple_of(lax.rem(mp_index + i, count) * wide, wide), wide)

    @pl.when(own >= 0)
    def _():
        arrivals = [(rows_hbm.at[:, place(j)], 0, j) for j in range(count)]
        for i, source in enumerate((one_hbm, two_hbm, three_hbm)):
            arrivals.append((source.at[:, block(0)], i + 1, i + 1))
            arrivals.append((source.at[:, block(1)], i + 1, (i + 1) % (count - 1) + 1))
        copies = [
            pltpu.make_async_copy(source, m_ref.at[block(i), block(j)], in_sems.at[at])
            for at, (source, i, j) in enumerate(arrivals)
        ]
        for copy in copies:
            copy.start()

        traces = jnp.sum(traces_ref[...], axis=0, keepdims=True)
        lane_ids = lax.broadcasted_iota(jnp.int32, traces.shape, 1)

        def pick_lane(lane):
            return jnp.sum(jnp.where(lane_ids == lane, traces, 0.0), axis=1, keepdims=True)

        lane = 2 * layer
        ratio = jnp.sqrt(pick_lane(lane) / FF / (pick_lane(lane + 1) / D))
        shift = jnp.where(lax.rem(own, layer_blocks) < a_span, DAMPING_BASE * ratio, DAMPING_BASE / ratio)
        diagonal = lax.broadcasted_iota(jnp.int32, (wide, wide), 0) == lax.broadcasted_iota(
            jnp.int32, (wide, wide), 1
        )
        for copy in copies:
            copy.wait()

        for _, i, j in arrivals:
            value = m_ref[block(i), block(j)]
            if i == j:
                m_ref[block(i), block(i)] = jnp.where(diagonal, value + shift, value)
            else:
                m_ref[block(j), block(i)] = value.T

        @pl.loop(0, count)
        def _(k):
            at = pl.ds(pl.multiple_of(k * wide, wide), wide)
            d_ref[...] = m_ref[at, at]
            block_sweep(d_ref)

            left_ref[...] = stacked(m_ref[:, at], LEFT, 1)
            right_ref[...] = stacked(m_ref[at, :], RIGHT, 0)
            rows = -dot(stacked(d_ref[...], LEFT, 1), right_ref[...])
            m_ref[:, at] = jnp.zeros((n, wide), jnp.float32)
            m_ref[at, :] = rows
            m_ref[at, at] = d_ref[...]
            right_ref[...] = stacked(m_ref[at, :], RIGHT, 0)
            left_ref[at, :] = jnp.zeros((wide, 3 * wide), jnp.bfloat16)
            for j in range(count):
                m_ref[:, block(j)] = m_ref[:, block(j)] - dot(left_ref[...], right_ref[:, block(j)])

        for j in range(count):
            band = (-m_ref[block(0), block(j)]).astype(jnp.bfloat16)
            for r in range(wide // ROWS):
                for c in range(wide // LANES):
                    at = lax.rem(mp_index + j, count) * (wide // LANES) + r * (n // LANES) + c
                    band_ref[at] = band[r * ROWS : (r + 1) * ROWS, c * LANES : (c + 1) * LANES]
        sent = pltpu.make_async_copy(band_ref, band_hbm, out_sem)
        sent.start()
        for j in range(count):
            for i in range(count):
                full_ref[place(i), place(j)] = (-m_ref[block(i), block(j)]).astype(jnp.bfloat16)
        sent.wait()

    @pl.when(own < 0)
    def _():
        band_ref[...] = jnp.zeros(band_ref.shape, jnp.bfloat16)
        full_ref[...] = jnp.zeros(full_ref.shape, jnp.bfloat16)
        sent = pltpu.make_async_copy(band_ref, band_hbm, out_sem)
        sent.start()
        sent.wait()


def invert(slots, traces, rows, one, two, three):
    wide, n = rows.shape
    in_smem = pl.BlockSpec(memory_space=pltpu.SMEM)
    in_vmem = pl.BlockSpec(memory_space=pltpu.VMEM)
    in_hbm = pl.BlockSpec(memory_space=pltpu.HBM)
    pieces = (wide * n // (ROWS * LANES), ROWS, LANES)
    return pl.pallas_call(
        invert_kernel,
        out_shape=(
            jax.ShapeDtypeStruct(pieces, jnp.bfloat16),
            jax.ShapeDtypeStruct((n, n), jnp.bfloat16),
        ),
        in_specs=[in_smem, in_vmem] + [in_hbm] * 4,
        out_specs=(in_hbm, in_vmem),
        scratch_shapes=[
            pltpu.VMEM((n, n), jnp.float32),
            pltpu.VMEM((wide, wide), jnp.float32),
            pltpu.VMEM((n, 3 * wide), jnp.bfloat16),
            pltpu.VMEM((3 * wide, n), jnp.bfloat16),
            pltpu.VMEM(pieces, jnp.bfloat16),
            pltpu.SemaphoreType.DMA((10,)),
            pltpu.SemaphoreType.DMA,
        ],
        compiler_params=pltpu.CompilerParams(vmem_limit_bytes=56 * 1024 * 1024),
        cost_estimate=pl.CostEstimate(
            flops=36 * n * n * n, bytes_accessed=6 * n * n, transcendentals=0
        ),
    )(slots, traces, rows, one, two, three)


def prepare_kernel(mp_ref, rows_ref, near_ref, far_ref, trace_ref):
    wide, n = rows_ref.shape

    def place(i):
        return pl.ds(pl.multiple_of(lax.rem(mp_ref[0] + i, n // wide) * wide, wide), wide)

    own = rows_ref[:, place(0)]
    diagonal = lax.broadcasted_iota(jnp.int32, own.shape, 0) == lax.broadcasted_iota(
        jnp.int32, own.shape, 1
    )
    trace = jnp.sum(jnp.where(diagonal, own, 0.0), axis=0, keepdims=True)
    trace = jnp.sum(trace, axis=1, keepdims=True)
    trace_ref[...] = jnp.broadcast_to(trace[None], trace_ref.shape)
    near_ref[:, :wide] = own
    near_ref[:, wide:] = rows_ref[:, place(1)]
    far_ref[:, :wide] = own
    far_ref[:, wide:] = rows_ref[:, place(2)]


def prepare(mp_index, rows, copies):
    wide, n = rows.shape
    in_vmem = pl.BlockSpec(memory_space=pltpu.VMEM)
    return pl.pallas_call(
        prepare_kernel,
        out_shape=(
            jax.ShapeDtypeStruct((wide, 2 * wide), jnp.float32),
            jax.ShapeDtypeStruct((wide, 2 * wide), jnp.float32),
            jax.ShapeDtypeStruct((copies, 1, LANES), jnp.float32),
        ),
        in_specs=[pl.BlockSpec(memory_space=pltpu.SMEM), in_vmem],
        out_specs=(in_vmem,) * 3,
        compiler_params=pltpu.CompilerParams(vmem_limit_bytes=8 * 1024 * 1024),
    )(mp_index.reshape(1).astype(jnp.int32), rows)


def pick_kernel(index_ref, src_ref, out_ref):
    @pl.loop(0, out_ref.shape[0], unroll=8)
    def _(i):
        out_ref[i] = src_ref[index_ref[i]]


def pick(index, source):
    in_vmem = pl.BlockSpec(memory_space=pltpu.VMEM)
    return pl.pallas_call(
        pick_kernel,
        out_shape=jax.ShapeDtypeStruct(index.shape + source.shape[1:], source.dtype),
        in_specs=[pl.BlockSpec(memory_space=pltpu.SMEM), in_vmem],
        out_specs=in_vmem,
        compiler_params=pltpu.CompilerParams(vmem_limit_bytes=4 * 1024 * 1024),
    )(index, source)


def take(source, index):
    return source.at[index].get(mode="promise_in_bounds")


def positions(slot_ids, wanted):
    slot_range = jnp.arange(slot_ids.shape[0], dtype=jnp.int32)
    hit = slot_ids[None, :] == wanted[:, None]
    return jnp.sum(jnp.where(hit, slot_range[None, :], 0), axis=1).astype(jnp.int32)


def exchange(pieces, axes):
    return lax.all_to_all(pieces, axes, split_axis=0, concat_axis=0, tiled=True)


def from_ahead(value, axis, step):
    count = lax.axis_size(axis)
    return lax.ppermute(value, axis, [((i + step) % count, i) for i in range(count)])


def local(old_factors, gradients, old_slots, new_slots):
    mp_index = lax.axis_index("mp")
    mp_count = lax.axis_size("mp")
    z_count, x_count, c_count = lax.axis_size("z"), lax.axis_size("x"), lax.axis_size("c")
    z, x, c = lax.axis_index("z"), lax.axis_index("x"), lax.axis_index("c")
    dp_count = z_count * x_count * c_count
    dp_index = (z * x_count + x) * c_count + c
    band, width = old_factors.shape[2:]
    tile_count, row_count = gradients.shape[1:3]
    a_span = FF // width
    layer_blocks = a_span + D // width
    old_flat = old_slots.reshape(dp_count)
    new_flat = new_slots.reshape(dp_count)

    rows = old_factors[0, 0]
    near, far, trace = prepare(mp_index, rows, x_count * c_count * mp_count)
    trace = exchange(trace, ("x", "c", "mp")).reshape(x_count * c_count, mp_count, LANES)
    plane = lax.dynamic_slice_in_dim(old_flat, z * x_count * c_count, x_count * c_count)
    plane_bin = 2 * (plane // layer_blocks) + jnp.where(plane % layer_blocks < a_span, 0, 1)
    plane_bin = jnp.where(plane >= 0, plane_bin, -1)
    lane_ids = lax.broadcasted_iota(jnp.int32, (1, 1, LANES), 2)
    binned = jnp.sum(jnp.where(lane_ids == plane_bin[:, None, None], trace, 0.0), axis=(0, 1))
    binned, near, far, tiles = lax.optimization_barrier((binned, near, far, gradients[0]))
    binned = jnp.broadcast_to(binned[None, None], (z_count, 1, LANES))
    traces = exchange(binned, "z").reshape(z_count, LANES)

    one = from_ahead(near, "mp", 1)
    two = from_ahead(near, "mp", 2)
    three = from_ahead(far, "mp", 3)

    block = jnp.maximum(old_flat, 0)
    tile_of = jnp.minimum(block // layer_blocks * a_span + block % layer_blocks, tile_count - 1)
    tile_of = tile_of.reshape(z_count * x_count, c_count)

    def tiles_of(core):
        return take(tiles, lax.dynamic_index_in_dim(tile_of, core, 1, keepdims=False))

    arrived = from_ahead(tiles_of(1 - c), "c", 1)
    partial = tiles_of(c).astype(jnp.float32) + arrived.astype(jnp.float32)
    partial, traces = lax.optimization_barrier((partial.astype(jnp.bfloat16), traces))
    partial = exchange(partial, ("z", "x"))
    tile = jnp.sum(partial.astype(jnp.float32), axis=0).astype(jnp.bfloat16)

    places = jnp.stack([dp_index.astype(jnp.int32), mp_index.astype(jnp.int32)])
    slots = jnp.concatenate([old_flat, places])
    inverse_band, inverse = invert(slots, traces, rows, one, two, three)
    inverse_band, tile = lax.optimization_barrier((inverse_band, tile))

    def gather(value, axis, steps):
        return jnp.stack([value] + [from_ahead(value, axis, step) for step in steps])

    held = jnp.dot(tile, inverse, preferred_element_type=jnp.float32).astype(jnp.bfloat16)
    held = lax.all_gather(held, "z", axis=0, tiled=False)
    spread = exchange(inverse_band, DP)
    slot_range = jnp.arange(dp_count, dtype=jnp.int32)
    empty = jnp.min(jnp.where(old_flat >= 0, dp_count - 1, slot_range))
    source = jnp.where(new_flat >= 0, positions(old_flat, new_flat), empty)
    outgoing, held = lax.optimization_barrier((pick(source, spread), held))
    arrived = exchange(outgoing, DP)
    arrived = arrived.reshape(band // ROWS, width // LANES, ROWS, LANES)
    inverses = arrived.transpose(0, 2, 1, 3).reshape(1, 1, band, width)
    held = gather(gather(held, "x", (1, 2, 3)), "c", (1,))
    held = held.reshape(dp_count, row_count, width)
    tile_range = jnp.arange(tile_count, dtype=jnp.int32)
    place = positions(old_flat, tile_range // a_span * layer_blocks + tile_range % a_span)
    far_x = (place // c_count - x + x_count) % x_count
    far_c = (place - c + c_count) % c_count
    from_z = place // (x_count * c_count)
    precond = take(held, (far_c * x_count + far_x) * z_count + from_z)
    return (inverses, precond)


def solution(mesh):
    dp_count, mp_count = mesh.devices.shape
    z_count = dp_count // (X_COUNT * CORES)
    parts = Mesh(
        mesh.devices.reshape(z_count, X_COUNT, CORES, mp_count), DP + ("mp",)
    )
    in_specs = (P(DP, None, "mp", None), P(DP, None, "mp", None), P(), P())
    out_specs = (P(DP, None, "mp", None), P(None, "mp", None))
    return jax.shard_map(local, mesh=parts, in_specs=in_specs, out_specs=out_specs, check_vma=False)
```

```python
import jax
import jax.numpy as jnp
from jax import lax
from jax.experimental import pallas as pl
from jax.experimental.pallas import tpu as pltpu
from jax.sharding import Mesh, PartitionSpec as P

D = 8192
FF = 28672
DAMPING_BASE = 2.0
X_COUNT, CORES = 4, 2
DP = ("z", "x", "c")

BASE = 64
SUB = 8
ROWS, LANES = 16, 128


def row_of(x, j):
    return jnp.broadcast_to(x[j : j + 1, :], x.shape)


def lane_of(x, j):
    return jnp.broadcast_to(x[:, j : j + 1], x.shape)


def reciprocal(x):
    return pltpu.reciprocal(x, approx=True)


def halves(x):
    high = x.astype(jnp.bfloat16)
    return high, (x - high.astype(jnp.float32)).astype(jnp.bfloat16)


def stacked(x, order, axis):
    parts = halves(x)
    return jnp.concatenate([parts[i] for i in order], axis=axis)


LEFT, RIGHT = (0, 0, 1), (0, 1, 0)


def dot(left, right):
    return jnp.dot(left, right, preferred_element_type=jnp.float32)


def panel_sweep(groups, first):
    sub_ids = lax.broadcasted_iota(jnp.int32, (SUB, LANES), 0)
    lane_ids = lax.broadcasted_iota(jnp.int32, (SUB, LANES), 1)
    for p in range(len(groups)):
        tile, lane = divmod(first + p * SUB, LANES)
        pivot_lanes = (lane_ids // SUB) == lane // SUB
        spread = [lane_of(groups[p][tile], lane + j) for j in range(SUB)]
        rows = list(groups[p])
        rows[tile] = jnp.where(
            pivot_lanes, jnp.where(lane_ids == sub_ids + lane, 1.0, 0.0), rows[tile]
        )
        pivot = row_of(spread[0], 0)
        for j in range(SUB):
            here = sub_ids == j
            scale = reciprocal(pivot)
            if j + 1 < SUB:
                cross = row_of(spread[j], j + 1) * row_of(spread[j + 1], j)
                pivot = row_of(spread[j + 1], j + 1) - cross * scale
            column = jnp.where(here, -1.0, spread[j])

            def eliminate(x):
                line = row_of(x, j)
                return jnp.where(here, 0.0, x) - (column * line) * scale

            rows = [eliminate(x) for x in rows]
            for i in range(j + 1, SUB):
                spread[i] = eliminate(spread[i])
        rows[tile] = jnp.where(pivot_lanes, -rows[tile], rows[tile])
        lines = [[row_of(x, j) for x in rows] for j in range(SUB)]
        for g in range(len(groups)):
            if g == p:
                continue
            factors = [lane_of(groups[g][tile], lane + j) for j in range(SUB)]
            for t in range(len(rows)):
                terms = [factors[j] * lines[j][t] for j in range(SUB)]
                while len(terms) > 1:
                    terms = [a + b for a, b in zip(terms[::2], terms[1::2])]
                kept = groups[g][t]
                if t == tile:
                    kept = jnp.where(pivot_lanes, 0.0, kept)
                groups[g][t] = kept - terms[0]
        groups[p] = rows
    return groups


def block_sweep(d_ref):
    wide = d_ref.shape[0]
    lane_ids = lax.broadcasted_iota(jnp.int32, (wide, wide), 1)
    for first in range(0, wide, BASE):
        old = d_ref[first : first + BASE, :]
        groups = [
            [old[g : g + SUB, t : t + LANES] for t in range(0, wide, LANES)]
            for g in range(0, BASE, SUB)
        ]
        groups = panel_sweep(groups, first)
        new = jnp.concatenate([jnp.concatenate(g, axis=1) for g in groups], axis=0)
        update = lax.dot_general(
            stacked(old, LEFT, 0),
            stacked(new, RIGHT, 0),
            (((0,), (0,)), ((), ())),
            preferred_element_type=jnp.float32,
        )
        kept = jnp.where(lane_ids // BASE == first // BASE, 0.0, d_ref[...])
        d_ref[...] = kept - update
        d_ref[first : first + BASE, :] = new


def invert_kernel(
    slots_ref, traces_ref, rows_hbm, one_hbm, two_hbm, three_hbm,
    band_hbm, full_ref, m_ref, d_ref, left_ref, right_ref, band_ref, in_sems, out_sem,
):
    wide, n = rows_hbm.shape
    count = n // wide
    dp_index, mp_index = slots_ref[slots_ref.shape[0] - 2], slots_ref[slots_ref.shape[0] - 1]
    own = slots_ref[dp_index]
    a_span = FF // n
    layer_blocks = a_span + D // n
    layer = lax.div(own, layer_blocks)

    def block(i):
        return slice(i * wide, (i + 1) * wide)

    def place(i):
        return pl.ds(pl.multiple_of(lax.rem(mp_index + i, count) * wide, wide), wide)

    @pl.when(own >= 0)
    def _():
        arrivals = [(rows_hbm.at[:, place(j)], 0, j) for j in range(count)]
        for i, source in enumerate((one_hbm, two_hbm, three_hbm)):
            arrivals.append((source.at[:, block(0)], i + 1, i + 1))
            arrivals.append((source.at[:, block(1)], i + 1, (i + 1) % (count - 1) + 1))
        copies = [
            pltpu.make_async_copy(source, m_ref.at[block(i), block(j)], in_sems.at[at])
            for at, (source, i, j) in enumerate(arrivals)
        ]
        for copy in copies:
            copy.start()

        traces = jnp.sum(traces_ref[...], axis=0, keepdims=True)
        lane_ids = lax.broadcasted_iota(jnp.int32, traces.shape, 1)

        def pick_lane(lane):
            return jnp.sum(jnp.where(lane_ids == lane, traces, 0.0), axis=1, keepdims=True)

        lane = 2 * layer
        ratio = jnp.sqrt(pick_lane(lane) / FF / (pick_lane(lane + 1) / D))
        shift = jnp.where(lax.rem(own, layer_blocks) < a_span, DAMPING_BASE * ratio, DAMPING_BASE / ratio)
        diagonal = lax.broadcasted_iota(jnp.int32, (wide, wide), 0) == lax.broadcasted_iota(
            jnp.int32, (wide, wide), 1
        )
        for copy in copies:
            copy.wait()

        for _, i, j in arrivals:
            value = m_ref[block(i), block(j)]
            if i == j:
                m_ref[block(i), block(i)] = jnp.where(diagonal, value + shift, value)
            else:
                m_ref[block(j), block(i)] = value.T

        @pl.loop(0, count)
        def _(k):
            at = pl.ds(pl.multiple_of(k * wide, wide), wide)
            d_ref[...] = m_ref[at, at]
            block_sweep(d_ref)

            left_ref[...] = stacked(m_ref[:, at], LEFT, 1)
            right_ref[...] = stacked(m_ref[at, :], RIGHT, 0)
            rows = -dot(stacked(d_ref[...], LEFT, 1), right_ref[...])
            m_ref[:, at] = jnp.zeros((n, wide), jnp.float32)
            m_ref[at, :] = rows
            m_ref[at, at] = d_ref[...]
            right_ref[...] = stacked(m_ref[at, :], RIGHT, 0)
            left_ref[at, :] = jnp.zeros((wide, 3 * wide), jnp.bfloat16)
            for j in range(count):
                m_ref[:, block(j)] = m_ref[:, block(j)] - dot(left_ref[...], right_ref[:, block(j)])

        for j in range(count):
            band = (-m_ref[block(0), block(j)]).astype(jnp.bfloat16)
            for r in range(wide // ROWS):
                for c in range(wide // LANES):
                    at = lax.rem(mp_index + j, count) * (wide // LANES) + r * (n // LANES) + c
                    band_ref[at] = band[r * ROWS : (r + 1) * ROWS, c * LANES : (c + 1) * LANES]
        sent = pltpu.make_async_copy(band_ref, band_hbm, out_sem)
        sent.start()
        for j in range(count):
            for i in range(count):
                full_ref[place(i), place(j)] = (-m_ref[block(i), block(j)]).astype(jnp.bfloat16)
        sent.wait()

    @pl.when(own < 0)
    def _():
        band_ref[...] = jnp.zeros(band_ref.shape, jnp.bfloat16)
        full_ref[...] = jnp.zeros(full_ref.shape, jnp.bfloat16)
        sent = pltpu.make_async_copy(band_ref, band_hbm, out_sem)
        sent.start()
        sent.wait()


def invert(slots, traces, rows, one, two, three):
    wide, n = rows.shape
    in_smem = pl.BlockSpec(memory_space=pltpu.SMEM)
    in_vmem = pl.BlockSpec(memory_space=pltpu.VMEM)
    in_hbm = pl.BlockSpec(memory_space=pltpu.HBM)
    pieces = (wide * n // (ROWS * LANES), ROWS, LANES)
    return pl.pallas_call(
        invert_kernel,
        out_shape=(
            jax.ShapeDtypeStruct(pieces, jnp.bfloat16),
            jax.ShapeDtypeStruct((n, n), jnp.bfloat16),
        ),
        in_specs=[in_smem, in_vmem] + [in_hbm] * 4,
        out_specs=(in_hbm, in_vmem),
        scratch_shapes=[
            pltpu.VMEM((n, n), jnp.float32),
            pltpu.VMEM((wide, wide), jnp.float32),
            pltpu.VMEM((n, 3 * wide), jnp.bfloat16),
            pltpu.VMEM((3 * wide, n), jnp.bfloat16),
            pltpu.VMEM(pieces, jnp.bfloat16),
            pltpu.SemaphoreType.DMA((10,)),
            pltpu.SemaphoreType.DMA,
        ],
        compiler_params=pltpu.CompilerParams(vmem_limit_bytes=56 * 1024 * 1024),
        cost_estimate=pl.CostEstimate(
            flops=36 * n * n * n, bytes_accessed=6 * n * n, transcendentals=0
        ),
    )(slots, traces, rows, one, two, three)


def prepare_kernel(mp_ref, rows_ref, near_ref, far_ref, trace_ref):
    wide, n = rows_ref.shape

    def place(i):
        return pl.ds(pl.multiple_of(lax.rem(mp_ref[0] + i, n // wide) * wide, wide), wide)

    own = rows_ref[:, place(0)]
    diagonal = lax.broadcasted_iota(jnp.int32, own.shape, 0) == lax.broadcasted_iota(
        jnp.int32, own.shape, 1
    )
    trace = jnp.sum(jnp.where(diagonal, own, 0.0), axis=0, keepdims=True)
    trace = jnp.sum(trace, axis=1, keepdims=True)
    trace_ref[...] = jnp.broadcast_to(trace[None], trace_ref.shape)
    near_ref[:, :wide] = own
    near_ref[:, wide:] = rows_ref[:, place(1)]
    far_ref[:, :wide] = own
    far_ref[:, wide:] = rows_ref[:, place(2)]


def prepare(mp_index, rows, copies):
    wide, n = rows.shape
    in_vmem = pl.BlockSpec(memory_space=pltpu.VMEM)
    return pl.pallas_call(
        prepare_kernel,
        out_shape=(
            jax.ShapeDtypeStruct((wide, 2 * wide), jnp.float32),
            jax.ShapeDtypeStruct((wide, 2 * wide), jnp.float32),
            jax.ShapeDtypeStruct((copies, 1, LANES), jnp.float32),
        ),
        in_specs=[pl.BlockSpec(memory_space=pltpu.SMEM), in_vmem],
        out_specs=(in_vmem,) * 3,
        compiler_params=pltpu.CompilerParams(vmem_limit_bytes=8 * 1024 * 1024),
    )(mp_index.reshape(1).astype(jnp.int32), rows)


def pick_kernel(index_ref, src_ref, out_ref):
    @pl.loop(0, out_ref.shape[0], unroll=8)
    def _(i):
        out_ref[i] = src_ref[index_ref[i]]


def pick(index, source):
    in_vmem = pl.BlockSpec(memory_space=pltpu.VMEM)
    return pl.pallas_call(
        pick_kernel,
        out_shape=jax.ShapeDtypeStruct(index.shape + source.shape[1:], source.dtype),
        in_specs=[pl.BlockSpec(memory_space=pltpu.SMEM), in_vmem],
        out_specs=in_vmem,
        compiler_params=pltpu.CompilerParams(vmem_limit_bytes=4 * 1024 * 1024),
    )(index, source)


def take(source, index):
    return source.at[index].get(mode="promise_in_bounds")


def positions(slot_ids, wanted):
    slot_range = jnp.arange(slot_ids.shape[0], dtype=jnp.int32)
    hit = slot_ids[None, :] == wanted[:, None]
    return jnp.sum(jnp.where(hit, slot_range[None, :], 0), axis=1).astype(jnp.int32)


def exchange(pieces, axes):
    return lax.all_to_all(pieces, axes, split_axis=0, concat_axis=0, tiled=True)


def from_ahead(value, axis, step):
    count = lax.axis_size(axis)
    return lax.ppermute(value, axis, [((i + step) % count, i) for i in range(count)])


def local(old_factors, gradients, old_slots, new_slots):
    mp_index = lax.axis_index("mp")
    mp_count = lax.axis_size("mp")
    z_count, x_count, c_count = lax.axis_size("z"), lax.axis_size("x"), lax.axis_size("c")
    z, x, c = lax.axis_index("z"), lax.axis_index("x"), lax.axis_index("c")
    dp_count = z_count * x_count * c_count
    dp_index = (z * x_count + x) * c_count + c
    band, width = old_factors.shape[2:]
    tile_count, row_count = gradients.shape[1:3]
    a_span = FF // width
    layer_blocks = a_span + D // width
    old_flat = old_slots.reshape(dp_count)
    new_flat = new_slots.reshape(dp_count)

    rows = old_factors[0, 0]
    near, far, trace = prepare(mp_index, rows, x_count * c_count * mp_count)
    trace = exchange(trace, ("x", "c", "mp")).reshape(x_count * c_count, mp_count, LANES)
    plane = lax.dynamic_slice_in_dim(old_flat, z * x_count * c_count, x_count * c_count)
    plane_bin = 2 * (plane // layer_blocks) + jnp.where(plane % layer_blocks < a_span, 0, 1)
    plane_bin = jnp.where(plane >= 0, plane_bin, -1)
    lane_ids = lax.broadcasted_iota(jnp.int32, (1, 1, LANES), 2)
    binned = jnp.sum(jnp.where(lane_ids == plane_bin[:, None, None], trace, 0.0), axis=(0, 1))
    binned, near, far, tiles = lax.optimization_barrier((binned, near, far, gradients[0]))
    binned = jnp.broadcast_to(binned[None, None], (z_count, 1, LANES))
    traces = exchange(binned, "z").reshape(z_count, LANES)

    one = from_ahead(near, "mp", 1)
    two = from_ahead(near, "mp", 2)
    three = from_ahead(far, "mp", 3)

    block = jnp.maximum(old_flat, 0)
    tile_of = jnp.minimum(block // layer_blocks * a_span + block % layer_blocks, tile_count - 1)
    tile_of = tile_of.reshape(z_count * x_count, c_count)

    def tiles_of(core):
        return take(tiles, lax.dynamic_index_in_dim(tile_of, core, 1, keepdims=False))

    arrived = from_ahead(tiles_of(1 - c), "c", 1)
    partial = tiles_of(c).astype(jnp.float32) + arrived.astype(jnp.float32)
    partial, traces = lax.optimization_barrier((partial.astype(jnp.bfloat16), traces))
    partial = exchange(partial, ("z", "x"))
    tile = jnp.sum(partial.astype(jnp.float32), axis=0).astype(jnp.bfloat16)

    places = jnp.stack([dp_index.astype(jnp.int32), mp_index.astype(jnp.int32)])
    slots = jnp.concatenate([old_flat, places])
    inverse_band, inverse = invert(slots, traces, rows, one, two, three)
    inverse_band, tile = lax.optimization_barrier((inverse_band, tile))

    def gather(value, axis, steps):
        return jnp.stack([value] + [from_ahead(value, axis, step) for step in steps])

    held = jnp.dot(tile, inverse, preferred_element_type=jnp.float32).astype(jnp.bfloat16)
    held = lax.all_gather(held, "z", axis=0, tiled=False)
    spread = exchange(inverse_band, DP)
    slot_range = jnp.arange(dp_count, dtype=jnp.int32)
    empty = jnp.min(jnp.where(old_flat >= 0, dp_count - 1, slot_range))
    source = jnp.where(new_flat >= 0, positions(old_flat, new_flat), empty)
    outgoing, held = lax.optimization_barrier((pick(source, spread), held))
    arrived = exchange(outgoing, DP)
    arrived = arrived.reshape(band // ROWS, width // LANES, ROWS, LANES)
    inverses = arrived.transpose(0, 2, 1, 3).reshape(1, 1, band, width)
    held = gather(gather(held, "x", (1, 2, 3)), "c", (1,))
    held = held.reshape(dp_count, row_count, width)
    tile_range = jnp.arange(tile_count, dtype=jnp.int32)
    place = positions(old_flat, tile_range // a_span * layer_blocks + tile_range % a_span)
    far_x = (place // c_count - x + x_count) % x_count
    far_c = (place - c + c_count) % c_count
    from_z = place // (x_count * c_count)
    precond = take(held, (far_c * x_count + far_x) * z_count + from_z)
    return (inverses, precond)


def solution(mesh):
    dp_count, mp_count = mesh.devices.shape
    z_count = dp_count // (X_COUNT * CORES)
    parts = Mesh(
        mesh.devices.reshape(z_count, X_COUNT, CORES, mp_count), DP + ("mp",)
    )
    in_specs = (P(DP, None, "mp", None), P(DP, None, "mp", None), P(), P())
    out_specs = (P(DP, None, "mp", None), P(None, "mp", None))
    return jax.shard_map(local, mesh=parts, in_specs=in_specs, out_specs=out_specs, check_vma=False)
```

```python
import jax
import jax.numpy as jnp
from jax import lax
from jax.experimental import pallas as pl
from jax.experimental.pallas import tpu as pltpu
from jax.sharding import Mesh, PartitionSpec as P

D = 8192
FF = 28672
DAMPING_BASE = 2.0
X_COUNT, CORES = 4, 2
DP = ("z", "x", "c")

BASE = 32
SUB = 8
ROWS, LANES = 16, 128


def row_of(x, j):
    return jnp.broadcast_to(x[j : j + 1, :], x.shape)


def lane_of(x, j):
    return jnp.broadcast_to(x[:, j : j + 1], x.shape)


def reciprocal(x):
    return pltpu.reciprocal(x, approx=True)


def halves(x):
    high = x.astype(jnp.bfloat16)
    return high, (x - high.astype(jnp.float32)).astype(jnp.bfloat16)


def stacked(x, order, axis):
    parts = halves(x)
    return jnp.concatenate([parts[i] for i in order], axis=axis)


LEFT, RIGHT = (0, 0, 1), (0, 1, 0)


def dot(left, right):
    return jnp.dot(left, right, preferred_element_type=jnp.float32)


def panel_sweep(groups, first):
    sub_ids = lax.broadcasted_iota(jnp.int32, (SUB, LANES), 0)
    lane_ids = lax.broadcasted_iota(jnp.int32, (SUB, LANES), 1)
    for p in range(len(groups)):
        tile, lane = divmod(first + p * SUB, LANES)
        pivot_lanes = (lane_ids // SUB) == lane // SUB
        spread = [lane_of(groups[p][tile], lane + j) for j in range(SUB)]
        rows = list(groups[p])
        rows[tile] = jnp.where(
            pivot_lanes, jnp.where(lane_ids == sub_ids + lane, 1.0, 0.0), rows[tile]
        )
        pivot = row_of(spread[0], 0)
        for j in range(SUB):
            here = sub_ids == j
            scale = reciprocal(pivot)
            if j + 1 < SUB:
                cross = row_of(spread[j], j + 1) * row_of(spread[j + 1], j)
                pivot = row_of(spread[j + 1], j + 1) - cross * scale
            column = jnp.where(here, -1.0, spread[j])

            def eliminate(x):
                line = row_of(x, j)
                return jnp.where(here, 0.0, x) - (column * line) * scale

            rows = [eliminate(x) for x in rows]
            for i in range(j + 1, SUB):
                spread[i] = eliminate(spread[i])
        rows[tile] = jnp.where(pivot_lanes, -rows[tile], rows[tile])
        lines = [[row_of(x, j) for x in rows] for j in range(SUB)]
        for g in range(len(groups)):
            if g == p:
                continue
            factors = [lane_of(groups[g][tile], lane + j) for j in range(SUB)]
            for t in range(len(rows)):
                terms = [factors[j] * lines[j][t] for j in range(SUB)]
                while len(terms) > 1:
                    terms = [a + b for a, b in zip(terms[::2], terms[1::2])]
                kept = groups[g][t]
                if t == tile:
                    kept = jnp.where(pivot_lanes, 0.0, kept)
                groups[g][t] = kept - terms[0]
        groups[p] = rows
    return groups


def block_sweep(d_ref):
    wide = d_ref.shape[0]
    lane_ids = lax.broadcasted_iota(jnp.int32, (wide, wide), 1)
    for first in range(0, wide, BASE):
        old = d_ref[first : first + BASE, :]
        groups = [
            [old[g : g + SUB, t : t + LANES] for t in range(0, wide, LANES)]
            for g in range(0, BASE, SUB)
        ]
        groups = panel_sweep(groups, first)
        new = jnp.concatenate([jnp.concatenate(g, axis=1) for g in groups], axis=0)
        update = lax.dot_general(
            stacked(old, LEFT, 0),
            stacked(new, RIGHT, 0),
            (((0,), (0,)), ((), ())),
            preferred_element_type=jnp.float32,
        )
        kept = jnp.where(lane_ids // BASE == first // BASE, 0.0, d_ref[...])
        d_ref[...] = kept - update
        d_ref[first : first + BASE, :] = new


def invert_kernel(
    slots_ref, traces_ref, rows_hbm, one_hbm, two_hbm, three_hbm,
    band_hbm, full_ref, m_ref, d_ref, left_ref, right_ref, band_ref, in_sems, out_sem,
):
    wide, n = rows_hbm.shape
    count = n // wide
    dp_index, mp_index = slots_ref[slots_ref.shape[0] - 2], slots_ref[slots_ref.shape[0] - 1]
    own = slots_ref[dp_index]
    a_span = FF // n
    layer_blocks = a_span + D // n
    layer = lax.div(own, layer_blocks)

    def block(i):
        return slice(i * wide, (i + 1) * wide)

    def place(i):
        return pl.ds(pl.multiple_of(lax.rem(mp_index + i, count) * wide, wide), wide)

    @pl.when(own >= 0)
    def _():
        arrivals = [(rows_hbm.at[:, place(j)], 0, j) for j in range(count)]
        for i, source in enumerate((one_hbm, two_hbm, three_hbm)):
            arrivals.append((source.at[:, block(0)], i + 1, i + 1))
            arrivals.append((source.at[:, block(1)], i + 1, (i + 1) % (count - 1) + 1))
        copies = [
            pltpu.make_async_copy(source, m_ref.at[block(i), block(j)], in_sems.at[at])
            for at, (source, i, j) in enumerate(arrivals)
        ]
        for copy in copies:
            copy.start()

        traces = jnp.sum(traces_ref[...], axis=0, keepdims=True)
        lane_ids = lax.broadcasted_iota(jnp.int32, traces.shape, 1)

        def pick_lane(lane):
            return jnp.sum(jnp.where(lane_ids == lane, traces, 0.0), axis=1, keepdims=True)

        lane = 2 * layer
        ratio = jnp.sqrt(pick_lane(lane) / FF / (pick_lane(lane + 1) / D))
        shift = jnp.where(lax.rem(own, layer_blocks) < a_span, DAMPING_BASE * ratio, DAMPING_BASE / ratio)
        diagonal = lax.broadcasted_iota(jnp.int32, (wide, wide), 0) == lax.broadcasted_iota(
            jnp.int32, (wide, wide), 1
        )
        for copy in copies:
            copy.wait()

        for _, i, j in arrivals:
            value = m_ref[block(i), block(j)]
            if i == j:
                m_ref[block(i), block(i)] = jnp.where(diagonal, value + shift, value)
            else:
                m_ref[block(j), block(i)] = value.T

        @pl.loop(0, count)
        def _(k):
            at = pl.ds(pl.multiple_of(k * wide, wide), wide)
            d_ref[...] = m_ref[at, at]
            block_sweep(d_ref)

            left_ref[...] = stacked(m_ref[:, at], LEFT, 1)
            right_ref[...] = stacked(m_ref[at, :], RIGHT, 0)
            rows = -dot(stacked(d_ref[...], LEFT, 1), right_ref[...])
            m_ref[:, at] = jnp.zeros((n, wide), jnp.float32)
            m_ref[at, :] = rows
            m_ref[at, at] = d_ref[...]
            right_ref[...] = stacked(m_ref[at, :], RIGHT, 0)
            left_ref[at, :] = jnp.zeros((wide, 3 * wide), jnp.bfloat16)
            for j in range(count):
                m_ref[:, block(j)] = m_ref[:, block(j)] - dot(left_ref[...], right_ref[:, block(j)])

        for j in range(count):
            band = (-m_ref[block(0), block(j)]).astype(jnp.bfloat16)
            for r in range(wide // ROWS):
                for c in range(wide // LANES):
                    at = lax.rem(mp_index + j, count) * (wide // LANES) + r * (n // LANES) + c
                    band_ref[at] = band[r * ROWS : (r + 1) * ROWS, c * LANES : (c + 1) * LANES]
        sent = pltpu.make_async_copy(band_ref, band_hbm, out_sem)
        sent.start()
        for j in range(count):
            for i in range(count):
                full_ref[place(i), place(j)] = (-m_ref[block(i), block(j)]).astype(jnp.bfloat16)
        sent.wait()

    @pl.when(own < 0)
    def _():
        band_ref[...] = jnp.zeros(band_ref.shape, jnp.bfloat16)
        full_ref[...] = jnp.zeros(full_ref.shape, jnp.bfloat16)
        sent = pltpu.make_async_copy(band_ref, band_hbm, out_sem)
        sent.start()
        sent.wait()


def invert(slots, traces, rows, one, two, three):
    wide, n = rows.shape
    in_smem = pl.BlockSpec(memory_space=pltpu.SMEM)
    in_vmem = pl.BlockSpec(memory_space=pltpu.VMEM)
    in_hbm = pl.BlockSpec(memory_space=pltpu.HBM)
    pieces = (wide * n // (ROWS * LANES), ROWS, LANES)
    return pl.pallas_call(
        invert_kernel,
        out_shape=(
            jax.ShapeDtypeStruct(pieces, jnp.bfloat16),
            jax.ShapeDtypeStruct((n, n), jnp.bfloat16),
        ),
        in_specs=[in_smem, in_vmem] + [in_hbm] * 4,
        out_specs=(in_hbm, in_vmem),
        scratch_shapes=[
            pltpu.VMEM((n, n), jnp.float32),
            pltpu.VMEM((wide, wide), jnp.float32),
            pltpu.VMEM((n, 3 * wide), jnp.bfloat16),
            pltpu.VMEM((3 * wide, n), jnp.bfloat16),
            pltpu.VMEM(pieces, jnp.bfloat16),
            pltpu.SemaphoreType.DMA((10,)),
            pltpu.SemaphoreType.DMA,
        ],
        compiler_params=pltpu.CompilerParams(vmem_limit_bytes=56 * 1024 * 1024),
        cost_estimate=pl.CostEstimate(
            flops=36 * n * n * n, bytes_accessed=6 * n * n, transcendentals=0
        ),
    )(slots, traces, rows, one, two, three)


def prepare_kernel(mp_ref, rows_ref, near_ref, far_ref, trace_ref):
    wide, n = rows_ref.shape

    def place(i):
        return pl.ds(pl.multiple_of(lax.rem(mp_ref[0] + i, n // wide) * wide, wide), wide)

    own = rows_ref[:, place(0)]
    diagonal = lax.broadcasted_iota(jnp.int32, own.shape, 0) == lax.broadcasted_iota(
        jnp.int32, own.shape, 1
    )
    trace = jnp.sum(jnp.where(diagonal, own, 0.0), axis=0, keepdims=True)
    trace = jnp.sum(trace, axis=1, keepdims=True)
    trace_ref[...] = jnp.broadcast_to(trace[None], trace_ref.shape)
    near_ref[:, :wide] = own
    near_ref[:, wide:] = rows_ref[:, place(1)]
    far_ref[:, :wide] = own
    far_ref[:, wide:] = rows_ref[:, place(2)]


def prepare(mp_index, rows, copies):
    wide, n = rows.shape
    in_vmem = pl.BlockSpec(memory_space=pltpu.VMEM)
    return pl.pallas_call(
        prepare_kernel,
        out_shape=(
            jax.ShapeDtypeStruct((wide, 2 * wide), jnp.float32),
            jax.ShapeDtypeStruct((wide, 2 * wide), jnp.float32),
            jax.ShapeDtypeStruct((copies, 1, LANES), jnp.float32),
        ),
        in_specs=[pl.BlockSpec(memory_space=pltpu.SMEM), in_vmem],
        out_specs=(in_vmem,) * 3,
        compiler_params=pltpu.CompilerParams(vmem_limit_bytes=8 * 1024 * 1024),
    )(mp_index.reshape(1).astype(jnp.int32), rows)


def pick_kernel(index_ref, src_ref, out_ref):
    @pl.loop(0, out_ref.shape[0], unroll=8)
    def _(i):
        out_ref[i] = src_ref[index_ref[i]]


def pick(index, source):
    in_vmem = pl.BlockSpec(memory_space=pltpu.VMEM)
    return pl.pallas_call(
        pick_kernel,
        out_shape=jax.ShapeDtypeStruct(index.shape + source.shape[1:], source.dtype),
        in_specs=[pl.BlockSpec(memory_space=pltpu.SMEM), in_vmem],
        out_specs=in_vmem,
        compiler_params=pltpu.CompilerParams(vmem_limit_bytes=4 * 1024 * 1024),
    )(index, source)


def take(source, index):
    return source.at[index].get(mode="promise_in_bounds")


def positions(slot_ids, wanted):
    slot_range = jnp.arange(slot_ids.shape[0], dtype=jnp.int32)
    hit = slot_ids[None, :] == wanted[:, None]
    return jnp.sum(jnp.where(hit, slot_range[None, :], 0), axis=1).astype(jnp.int32)


def exchange(pieces, axes):
    return lax.all_to_all(pieces, axes, split_axis=0, concat_axis=0, tiled=True)


def from_ahead(value, axis, step):
    count = lax.axis_size(axis)
    return lax.ppermute(value, axis, [((i + step) % count, i) for i in range(count)])


def local(old_factors, gradients, old_slots, new_slots):
    mp_index = lax.axis_index("mp")
    mp_count = lax.axis_size("mp")
    z_count, x_count, c_count = lax.axis_size("z"), lax.axis_size("x"), lax.axis_size("c")
    z, x, c = lax.axis_index("z"), lax.axis_index("x"), lax.axis_index("c")
    dp_count = z_count * x_count * c_count
    dp_index = (z * x_count + x) * c_count + c
    band, width = old_factors.shape[2:]
    tile_count, row_count = gradients.shape[1:3]
    a_span = FF // width
    layer_blocks = a_span + D // width
    old_flat = old_slots.reshape(dp_count)
    new_flat = new_slots.reshape(dp_count)

    rows = old_factors[0, 0]
    near, far, trace = prepare(mp_index, rows, x_count * c_count * mp_count)
    trace = exchange(trace, ("x", "c", "mp")).reshape(x_count * c_count, mp_count, LANES)
    plane = lax.dynamic_slice_in_dim(old_flat, z * x_count * c_count, x_count * c_count)
    plane_bin = 2 * (plane // layer_blocks) + jnp.where(plane % layer_blocks < a_span, 0, 1)
    plane_bin = jnp.where(plane >= 0, plane_bin, -1)
    lane_ids = lax.broadcasted_iota(jnp.int32, (1, 1, LANES), 2)
    binned = jnp.sum(jnp.where(lane_ids == plane_bin[:, None, None], trace, 0.0), axis=(0, 1))
    binned, near, far = lax.optimization_barrier((binned, near, far))
    tiles = gradients[0]
    binned = jnp.broadcast_to(binned[None, None], (z_count, 1, LANES))
    traces = exchange(binned, "z").reshape(z_count, LANES)

    one = from_ahead(near, "mp", 1)
    two = from_ahead(near, "mp", 2)
    three = from_ahead(far, "mp", 3)

    block = jnp.maximum(old_flat, 0)
    tile_of = jnp.minimum(block // layer_blocks * a_span + block % layer_blocks, tile_count - 1)
    tile_of = tile_of.reshape(z_count * x_count, c_count)

    def tiles_of(core):
        return take(tiles, lax.dynamic_index_in_dim(tile_of, core, 1, keepdims=False))

    arrived = from_ahead(tiles_of(1 - c), "c", 1)
    partial = tiles_of(c).astype(jnp.float32) + arrived.astype(jnp.float32)
    partial, traces = lax.optimization_barrier((partial.astype(jnp.bfloat16), traces))
    partial = exchange(partial, ("z", "x"))
    tile = jnp.sum(partial.astype(jnp.float32), axis=0).astype(jnp.bfloat16)

    places = jnp.stack([dp_index.astype(jnp.int32), mp_index.astype(jnp.int32)])
    slots = jnp.concatenate([old_flat, places])
    inverse_band, inverse = invert(slots, traces, rows, one, two, three)
    inverse_band, tile = lax.optimization_barrier((inverse_band, tile))

    def gather(value, axis, steps):
        return jnp.stack([value] + [from_ahead(value, axis, step) for step in steps])

    held = jnp.dot(tile, inverse, preferred_element_type=jnp.float32).astype(jnp.bfloat16)
    held = lax.all_gather(held, "z", axis=0, tiled=False)
    spread = exchange(inverse_band, DP)
    slot_range = jnp.arange(dp_count, dtype=jnp.int32)
    empty = jnp.min(jnp.where(old_flat >= 0, dp_count - 1, slot_range))
    source = jnp.where(new_flat >= 0, positions(old_flat, new_flat), empty)
    outgoing, held = lax.optimization_barrier((pick(source, spread), held))
    arrived = exchange(outgoing, DP)
    arrived = arrived.reshape(band // ROWS, width // LANES, ROWS, LANES)
    inverses = arrived.transpose(0, 2, 1, 3).reshape(1, 1, band, width)
    held = gather(gather(held, "x", (1, 2, 3)), "c", (1,))
    held = held.reshape(dp_count, row_count, width)
    tile_range = jnp.arange(tile_count, dtype=jnp.int32)
    place = positions(old_flat, tile_range // a_span * layer_blocks + tile_range % a_span)
    far_x = (place // c_count - x + x_count) % x_count
    far_c = (place - c + c_count) % c_count
    from_z = place // (x_count * c_count)
    precond = take(held, (far_c * x_count + far_x) * z_count + from_z)
    return (inverses, precond)


def solution(mesh):
    dp_count, mp_count = mesh.devices.shape
    z_count = dp_count // (X_COUNT * CORES)
    parts = Mesh(
        mesh.devices.reshape(z_count, X_COUNT, CORES, mp_count), DP + ("mp",)
    )
    in_specs = (P(DP, None, "mp", None), P(DP, None, "mp", None), P(), P())
    out_specs = (P(DP, None, "mp", None), P(None, "mp", None))
    return jax.shard_map(local, mesh=parts, in_specs=in_specs, out_specs=out_specs, check_vma=False)
```
